128 devices in a mesh: grp: 4 (over y_lo, core), dev: 32 (over x, z, y_hi).
Axes of the slice: x: 4, y: 4 (y_hi: 2, y_lo: 2; y = y_hi * 2 + y_lo), z: 4, core: 2. Of those that a mesh axis runs over, the one named last changes fastest.
Arguments:
- tokens: bfloat16 [16384, 2048], P(('grp', 'dev')), may hold values from -6 to 6
- cotangent: bfloat16 [16384, 2048], P(('grp', 'dev')), may hold values from -1.5 to 1.5
- route_weight: float32 [16384, 2], P(('grp', 'dev')), may hold values from 0.1 to 1
- slot_expert: int32 [128], replicated, may hold values from 0 to 15, as said below
- targets: int32 [16384, 2], P(('grp', 'dev')), may hold values from 0 to 127, as said below
- proj_in: float32 [16, 2048, 2048], P('grp', 'dev'), may hold values from -0.125 to 0.125
- first_in: float32 [16, 2048, 2048], P('grp', 'dev'), may hold values from -6 to 6
- second_in: float32 [16, 2048, 2048], P('grp', 'dev'), may hold values from 0.01 to 1
- proj_out: float32 [16, 1024, 2048], P('grp', 'dev'), may hold values from -0.1875 to 0.1875
- first_out: float32 [16, 1024, 2048], P('grp', 'dev'), may hold values from -6 to 6
- second_out: float32 [16, 1024, 2048], P('grp', 'dev'), may hold values from 0.01 to 1
Outputs:
- mixed: bfloat16 [16384, 2048], P(('grp', 'dev'))
- token_grad: bfloat16 [16384, 2048], P(('grp', 'dev'))
- mix_grad: float32 [16384, 2], P(('grp', 'dev'))
- trained_in: float32 [16, 2048, 2048], P('grp', 'dev')
- mean_in: float32 [16, 2048, 2048], P('grp', 'dev')
- square_in: float32 [16, 2048, 2048], P('grp', 'dev')
- trained_out: float32 [16, 1024, 2048], P('grp', 'dev')
- mean_out: float32 [16, 1024, 2048], P('grp', 'dev')
- square_out: float32 [16, 1024, 2048], P('grp', 'dev')
The draws below stay inside these ranges and needn't reach their ends.
Inputs may be any that keep to these rules, and one draw needn't show every extreme that they name: `slot_expert`: entry s is the expert held by slot s, the device s in grp+dev order; each of the 16 experts is held by at least one slot. `targets`: entry [t, k] is the slot that serves the k-th expert of token t; the two slots of a token hold different experts.
All inputs are finite; a program needn't handle non-finite values.
Results may differ from the reference program's by a relative error of at most 0.015.
The reference program's roundings to bfloat16 on the way count: a program that leaves them out, or rounds other values in their place, can miss the bound.
Values may be sent and summed in bfloat16 or wider, within the bound.
No kernel may reach another device: no remote copies, remote signals or barrier semaphores. Data moves between devices by JAX's collectives and lax.ppermute only.
A program may use at most 128 MiB of HBM per device.

```python
import math
import jax
import jax.numpy as jnp
from jax import lax

D = 2048
FF = 1024
E = 16
TOK_DEV = 128
SLOTS = 128
TOKENS = 16384
CAP = 3
N_GRP = 4
N_DEV = 32


def route_plan(key):
    folded = jax.random.fold_in(key, 4243)
    subkeys = jax.random.split(folded, 6)
    shuffle = jax.random.permutation(subkeys[0], E)
    first_pick = jax.random.randint(subkeys[1], (SLOTS - E,), 0, E)
    second_pick = jax.random.randint(subkeys[2], (SLOTS - E,), 0, E)
    extras = shuffle[jnp.minimum(first_pick, second_pick)].astype(jnp.int32)
    filled = jnp.concatenate([jnp.arange(E, dtype=jnp.int32), extras])
    reorder = jax.random.permutation(subkeys[3], SLOTS)
    experts = filled[reorder].astype(jnp.int32)
    first_slot = jax.random.randint(subkeys[4], (TOKENS,), 0, SLOTS).astype(jnp.int32)
    first_expert = experts[first_slot]
    differ = (experts[None, :] != first_expert[:, None]).astype(jnp.int32)
    others = jnp.sum(differ, axis=1)
    chosen = jax.random.randint(subkeys[5], (TOKENS,), 0, others).astype(jnp.int32)
    running = jnp.cumsum(differ, axis=1)
    second_slot = jnp.sum((running <= chosen[:, None]).astype(jnp.int32), axis=1)
    return (experts, jnp.stack([first_slot, second_slot], axis=1).astype(jnp.int32))


def draw_slot_expert(key, part):
    return route_plan(key)[0]


def draw_targets(key, part):
    return route_plan(key)[1]


def level_of(stream_key, extent, cuts, low, high):
    gain = 1.0
    for dim, parts in cuts:
        heights = jax.random.uniform(jax.random.fold_in(jax.random.fold_in(stream_key, 6), dim), (parts,), jnp.float32, low / len(cuts), high / len(cuts))
        gain = gain * jnp.repeat(jnp.exp(heights), extent[dim] // parts).reshape((-1,) + (1,) * (len(extent) - 1 - dim))
    return gain


def bell_draw(rng, shape, scale, limit, cuts=(), kind=jnp.bfloat16):
    loudness = level_of(rng, shape, cuts, -0.22, 0.18) if cuts else 1.0
    drawn = jax.random.normal(rng, shape, jnp.float32) * scale * loudness
    return jnp.minimum(jnp.maximum(drawn, -limit), limit).astype(kind)


def setup_inputs(seed: int = 0) -> dict:
    splits = jax.random.split(jax.random.key(seed), 12)
    return {
        "tokens": bell_draw(splits[0], (TOKENS, D), 1.0, 6.0, ((0, 128),)),
        "cotangent": bell_draw(splits[1], (TOKENS, D), 0.25, 1.5, ((0, 128),)),
        "route_weight": jnp.clip(0.1 + 0.9 * jax.random.uniform(splits[2], (TOKENS, 2), jnp.float32) ** level_of(splits[2], (TOKENS, 2), ((0, 128),), -0.2, 0.2), 0.1, 1.0),
        "slot_expert": draw_slot_expert(jax.random.fold_in(splits[11], 71), 0),
        "targets": draw_targets(jax.random.fold_in(splits[11], 71), 0),
        "proj_in": bell_draw(splits[5], (E, D, 2 * FF), D ** -0.5, 0.125, ((0, 4), (1, 32)), jnp.float32),
        "first_in": bell_draw(splits[6], (E, D, 2 * FF), 1.0, 6.0, ((0, 4), (1, 32)), jnp.float32),
        "second_in": jnp.clip(jnp.exp(math.log(1.0) - 4.6051702 * jax.random.uniform(splits[7], (E, D, 2 * FF), jnp.float32) ** level_of(splits[7], (E, D, 2 * FF), ((0, 4), (1, 32)), -0.2, 0.2)), 0.01, 1.0),
        "proj_out": bell_draw(splits[8], (E, FF, D), FF ** -0.5, 0.1875, ((0, 4), (1, 32)), jnp.float32),
        "first_out": bell_draw(splits[9], (E, FF, D), 1.0, 6.0, ((0, 4), (1, 32)), jnp.float32),
        "second_out": jnp.clip(jnp.exp(math.log(1.0) - 4.6051702 * jax.random.uniform(splits[10], (E, FF, D), jnp.float32) ** level_of(splits[10], (E, FF, D), ((0, 4), (1, 32)), -0.2, 0.2)), 0.01, 1.0),
    }


beta_first = 0.9
beta_second = 0.95
learn_rate = 0.01
decay_rate = 0.1
adam_eps = 1e-08
bias_first = 1.0 - 0.9 ** 10
bias_second = 1.0 - 0.95 ** 10

def silu_parts(values):
    logistic = jax.nn.sigmoid(values)
    return (values * logistic, logistic * (1.0 + values * (1.0 - logistic)))

def slot_pass(rows_x, rows_dy, weight_up, weight_down):
    gate_up = jnp.dot(rows_x, weight_up, preferred_element_type=jnp.float32)
    gating = gate_up[:, :FF]
    upward = gate_up[:, FF:]
    active, derivative = silu_parts(gating)
    hidden = (active * upward).astype(jnp.bfloat16)
    result = jnp.dot(hidden, weight_down, preferred_element_type=jnp.float32).astype(jnp.bfloat16)
    dhidden = lax.dot_general(rows_dy, weight_down, (((1,), (1,)), ((), ())), preferred_element_type=jnp.float32)
    grad_gateup = jnp.concatenate([dhidden * upward * derivative, dhidden * active], axis=1).astype(jnp.bfloat16)
    rows_dx = lax.dot_general(grad_gateup, weight_up, (((1,), (1,)), ((), ())), preferred_element_type=jnp.float32).astype(jnp.bfloat16)
    grad_up = lax.dot_general(rows_x, grad_gateup, (((0,), (0,)), ((), ())), preferred_element_type=jnp.float32).astype(jnp.bfloat16)
    grad_down = lax.dot_general(hidden, rows_dy, (((0,), (0,)), ((), ())), preferred_element_type=jnp.float32).astype(jnp.bfloat16)
    return (result, rows_dx, grad_up, grad_down)

def adam_step(weight, moment, square, gradient):
    new_moment = beta_first * moment + (1.0 - beta_first) * gradient
    new_square = beta_second * square + (1.0 - beta_second) * gradient * gradient
    update = new_moment / bias_first / (jnp.sqrt(new_square / bias_second) + adam_eps) + decay_rate * weight
    return (weight - learn_rate * update, new_moment, new_square)

def reference(tokens, cotangent, route_weight, slot_expert, targets, proj_in, first_in, second_in, proj_out, first_out, second_out):
    assigns = 2 * TOK_DEV
    buffer_rows = SLOTS * CAP
    per_source = targets.reshape(SLOTS, assigns)
    slot_ids = jnp.arange(SLOTS, dtype=jnp.int32)
    onehot = (per_source[:, :, None] == slot_ids[None, None, :]).astype(jnp.int32)
    earlier = jnp.cumsum(onehot, axis=1) - onehot
    position = lax.optimization_barrier(jnp.sum(earlier * onehot, axis=2)).astype(jnp.int32)
    within = position < CAP
    landing = per_source * buffer_rows + slot_ids[:, None] * CAP + position
    landing = jnp.where(within, landing, SLOTS * buffer_rows).astype(jnp.int32)
    assign_ids = jnp.arange(SLOTS * assigns, dtype=jnp.int32)
    row_table = jnp.full((SLOTS * buffer_rows,), -1, jnp.int32).at[landing.reshape(-1)].set(assign_ids, mode='drop')
    row_table = row_table.reshape(SLOTS, buffer_rows)
    flat_weight = route_weight.reshape(-1)
    scaled = (flat_weight[:, None] * jnp.repeat(cotangent, 2, axis=0).astype(jnp.float32)).astype(jnp.bfloat16)

    def serve_slot(carried, slot_id):
        acc_up, acc_down, out_all, dx_all = carried
        entries = row_table[slot_id]
        filled = entries >= 0
        safe_ids = jnp.where(filled, entries, 0).astype(jnp.int32)
        rows_x = jnp.where(filled[:, None], tokens[safe_ids // 2], jnp.zeros((), tokens.dtype))
        rows_dy = jnp.where(filled[:, None], scaled[safe_ids], jnp.zeros((), scaled.dtype))
        expert = slot_expert[slot_id]
        weight_up = lax.dynamic_index_in_dim(proj_in, expert, 0, keepdims=False).astype(jnp.bfloat16)
        weight_down = lax.dynamic_index_in_dim(proj_out, expert, 0, keepdims=False).astype(jnp.bfloat16)
        result, rows_dx, grad_up, grad_down = slot_pass(rows_x, rows_dy, weight_up, weight_down)
        acc_up = acc_up.at[expert].add(grad_up.astype(jnp.float32))
        acc_down = acc_down.at[expert].add(grad_down.astype(jnp.float32))
        landing_row = jnp.where(filled, entries, 2 * TOKENS).astype(jnp.int32)
        out_all = out_all.at[landing_row].set(result, mode='drop')
        dx_all = dx_all.at[landing_row].set(rows_dx, mode='drop')
        return ((acc_up, acc_down, out_all, dx_all), None)
    total_up = jnp.zeros((E, D, 2 * FF), jnp.float32)
    total_down = jnp.zeros((E, FF, D), jnp.float32)
    out_all = jnp.zeros((2 * TOKENS, D), jnp.bfloat16)
    dx_all = jnp.zeros((2 * TOKENS, D), jnp.bfloat16)
    for group_id in range(N_GRP):
        start_up = jnp.zeros((E, D, 2 * FF), jnp.float32)
        start_down = jnp.zeros((E, FF, D), jnp.float32)
        slot_range = jnp.arange(group_id * N_DEV, (group_id + 1) * N_DEV, dtype=jnp.int32)
        finished, unused = lax.scan(serve_slot, (start_up, start_down, out_all, dx_all), slot_range)
        acc_up, acc_down, out_all, dx_all = finished
        total_up = total_up + lax.optimization_barrier(acc_up.astype(jnp.bfloat16)).astype(jnp.float32)
        total_down = total_down + lax.optimization_barrier(acc_down.astype(jnp.bfloat16)).astype(jnp.float32)
    out_float = out_all.reshape(TOKENS, 2, D).astype(jnp.float32)
    dx_pairs = dx_all.reshape(TOKENS, 2, D).astype(jnp.float32)
    mixed = (route_weight[:, 0:1] * out_float[:, 0] + route_weight[:, 1:2] * out_float[:, 1]).astype(jnp.bfloat16)
    token_grad = (dx_pairs[:, 0] + dx_pairs[:, 1]).astype(jnp.bfloat16)
    mix_grad = lax.optimization_barrier(jnp.sum(cotangent.astype(jnp.float32)[:, None, :] * out_float, axis=2))
    trained_in, mean_in, square_in = adam_step(proj_in, first_in, second_in, total_up)
    trained_out, mean_out, square_out = adam_step(proj_out, first_out, second_out, total_down)
    return (mixed, token_grad, mix_grad, trained_in, mean_in, square_in, trained_out, mean_out, square_out)
```

```python
import jax
import jax.numpy as jnp
from jax import lax
from jax.experimental import pallas as pl
from jax.experimental.pallas import tpu as pltpu
from jax.sharding import Mesh, PartitionSpec as P

D = 2048
FF = 1024
E = 16
CAP = 3
UNITS = 8
CHIPS = 64
ROWS = CHIPS * UNITS
HALF = 1024

BF = jnp.bfloat16
F32 = jnp.float32

beta_first = 0.9
beta_second = 0.95
learn_rate = 0.01
decay_rate = 0.1
adam_eps = 1e-08
bias_first = 1.0 - 0.9**10
bias_second = 1.0 - 0.95**10

CHIP_AXES = ("yl", "x", "z", "yh")
DEV_AXES = ("x", "z", "yh")
ALL_AXES = ("yl", "core", "x", "z", "yh")


def params(mib=48):
    return pltpu.CompilerParams(vmem_limit_bytes=mib * 2**20)


def adam_step(weight, moment, square, gradient):
    new_moment = beta_first * moment + (1.0 - beta_first) * gradient
    new_square = beta_second * square + (1.0 - beta_second) * gradient * gradient
    update = (
        new_moment / bias_first / (jnp.sqrt(new_square / bias_second) + adam_eps)
        + decay_rate * weight
    )
    return (weight - learn_rate * update, new_moment, new_square)


def dispatch_kernel(tcol, trow, ecol, erow, wrow, tok, cot, send, dest):
    sub = lax.broadcasted_iota(jnp.int32, (128, 128), 0).astype(F32)
    lane = lax.broadcasted_iota(jnp.int32, (128, 128), 1).astype(F32)
    one, zero = jnp.float32(1.0), jnp.float32(0.0)

    def down(mask, value):
        return jnp.sum(jnp.where(mask, value, zero), axis=0, keepdims=True)

    def across(mask, value):
        return jnp.sum(jnp.where(mask, value, zero), axis=1, keepdims=True)

    tc = [tcol[:, k : k + 1].astype(F32) for k in range(2)]
    tr = [trow[k : k + 1, :].astype(F32) for k in range(2)]
    ec, er = ecol[...].astype(F32), erow[...].astype(F32)
    chips_row = jnp.floor((CAP * down(ec == lane, one) + (UNITS - 1)) / UNITS)
    chips_col = jnp.floor((CAP * across(er == sub, one) + (UNITS - 1)) / UNITS)
    base_col = UNITS * across(lane < ec, chips_row) + CAP * across((ec == er) & (lane < sub), one)
    base_row = UNITS * down(sub < er, chips_col) + CAP * down((ec == er) & (sub < lane), one)
    dest_row = []
    for k in range(2):
        pos_row = down((tc[0] == tr[k]) & (sub < lane), one) + down((tc[1] == tr[k]) & (sub < lane), one)
        pos_col = across((tc[k] == tr[0]) & (lane < sub), one) + across((tc[k] == tr[1]) & (lane < sub), one)
        at_row = down(sub == tr[k], base_col)
        at_col = across(lane == tc[k], base_row)
        dest_row.append(jnp.where(pos_row < CAP, at_row + pos_row, 4.0 * ROWS))
        dest[:, k : k + 1] = jnp.where(pos_col < CAP, at_col + pos_col, 4.0 * ROWS)
    w0, w1 = wrow[0:1, :], wrow[1:2, :]
    for part in range(ROWS // 128):
        place = sub + 128.0 * part
        first, second = place == dest_row[0], place == dest_row[1]
        pick = jnp.where(first | second, one, zero).astype(BF)
        weight = across(first, w0) + across(second, w1)
        rows = slice(part * 128, part * 128 + 128)
        send[rows, :D] = jnp.dot(pick, tok[...], preferred_element_type=F32).astype(BF)
        send[rows, D:] = (jnp.dot(pick, cot[...], preferred_element_type=F32) * weight).astype(BF)


def dispatch(targets, slot_expert, route_weight, tokens, cotangent):
    return pl.pallas_call(
        dispatch_kernel,
        out_shape=(
            jax.ShapeDtypeStruct((ROWS, 2 * D), BF),
            jax.ShapeDtypeStruct((128, 2), F32),
        ),
        compiler_params=params(),
        name="dispatch",
    )(
        targets,
        targets.T,
        slot_expert.reshape(128, 1),
        slot_expert.reshape(1, 128),
        route_weight.T,
        tokens,
        cotangent,
    )


def combine_kernel(dest, weight, cot, back, mixed, grad, mix):
    place = lax.broadcasted_iota(jnp.int32, (128, ROWS), 1).astype(F32)
    first, second = place == dest[:, 0:1], place == dest[:, 1:2]
    one, zero = jnp.float32(1.0), jnp.float32(0.0)
    pick0 = jnp.where(first, one, zero).astype(BF)
    pick1 = jnp.where(second, one, zero).astype(BF)
    both = jnp.where(first | second, one, zero).astype(BF)
    w0, w1 = weight[:, 0:1], weight[:, 1:2]
    mix0 = jnp.zeros((128, 1), F32)
    mix1 = jnp.zeros((128, 1), F32)
    width = 512
    for c in range(D // width):
        cols = slice(c * width, (c + 1) * width)
        out0 = jnp.dot(pick0, back[:, cols], preferred_element_type=F32)
        out1 = jnp.dot(pick1, back[:, cols], preferred_element_type=F32)
        here = cot[:, cols].astype(F32)
        mixed[:, cols] = (w0 * out0 + w1 * out1).astype(BF)
        mix0 += jnp.sum(here * out0, axis=1, keepdims=True)
        mix1 += jnp.sum(here * out1, axis=1, keepdims=True)
        dcols = slice(D + c * width, D + (c + 1) * width)
        grad[:, cols] = jnp.dot(both, back[:, dcols], preferred_element_type=F32).astype(BF)
    mix[:, 0:1] = mix0
    mix[:, 1:2] = mix1


def combine(dest, route_weight, cotangent, back):
    return pl.pallas_call(
        combine_kernel,
        out_shape=(
            jax.ShapeDtypeStruct((128, D), BF),
            jax.ShapeDtypeStruct((128, D), BF),
            jax.ShapeDtypeStruct((128, 2), F32),
        ),
        compiler_params=params(),
        name="combine",
    )(dest, route_weight, cotangent, back)


def select_kernel(index, near, far, out):
    step = pl.program_id(0)
    for j in range(8):
        e = index[step * 8 + j]

        @pl.when(e < 8)
        def _():
            out[j] = near[jnp.minimum(e, 7)]

        @pl.when(e >= 8)
        def _():
            out[j] = far[jnp.maximum(e - 8, 0)]


def select_rows(index, near, far):
    n, r, c = near.shape
    return pl.pallas_call(
        select_kernel,
        grid_spec=pltpu.PrefetchScalarGridSpec(
            num_scalar_prefetch=1,
            grid=(4,),
            in_specs=[
                pl.BlockSpec((n, r, c), lambda i, s: (0, 0, 0)),
                pl.BlockSpec((n, r, c), lambda i, s: (0, 0, 0)),
            ],
            out_specs=pl.BlockSpec((8, r, c), lambda i, s: (i, 0, 0)),
        ),
        out_shape=jax.ShapeDtypeStruct((32, r, c), BF),
        compiler_params=params(),
        name="select_rows",
    )(index, near, far)


def sum_kernel(index, rows, out, total):
    total[...] = jnp.zeros_like(total)
    for d in range(32):
        e = index[d]
        total[e] += rows[d].astype(F32)
    out[...] = total[...].astype(BF)


def sum_rows(index, rows):
    n, r, c = rows.shape
    step = 16
    return pl.pallas_call(
        sum_kernel,
        grid_spec=pltpu.PrefetchScalarGridSpec(
            num_scalar_prefetch=1,
            grid=(r // step,),
            in_specs=[pl.BlockSpec((n, step, c), lambda i, s: (0, i, 0))],
            out_specs=pl.BlockSpec((E, step, c), lambda i, s: (0, i, 0)),
            scratch_shapes=[pltpu.VMEM((E, step, c), F32)],
        ),
        out_shape=jax.ShapeDtypeStruct((E, r, c), BF),
        compiler_params=params(),
        name="sum_rows",
    )(index, rows)


def dot(a, b):
    return jnp.dot(a, b, preferred_element_type=F32)


def dot_nt(a, b):
    return lax.dot_general(a, b, (((1,), (1,)), ((), ())), preferred_element_type=F32)


def dot_tn(a, b):
    return lax.dot_general(a, b, (((0,), (0,)), ((), ())), preferred_element_type=F32)


def over_core(v):
    return lax.ppermute(v, "core", [(0, 1), (1, 0)])


def over_y(v):
    return lax.ppermute(v, "yl", [(0, 1), (1, 0)])


def on_device(
    tokens,
    cotangent,
    route_weight,
    slot_expert,
    targets,
    proj_in,
    first_in,
    second_in,
    proj_out,
    first_out,
    second_out,
):
    core = lax.axis_index("core")
    yl = lax.axis_index("yl")
    is0 = core == 0

    def half_of(v, which):
        return lax.dynamic_slice_in_dim(v, which * HALF, HALF, axis=v.ndim - 1)

    near, far = [], []
    for w in (proj_in, proj_out):
        low = w.astype(BF)
        mine = half_of(low, core)
        theirs = over_core(half_of(low, 1 - core))
        both = jnp.concatenate([mine, theirs], axis=0)
        near.append(both)
        far.append(over_y(both))

    ids = jnp.arange(E, dtype=jnp.int32)
    count = jnp.sum((slot_expert[:, None] == ids[None, :]).astype(jnp.int32), axis=0)
    chips = (CAP * count + UNITS - 1) // UNITS
    start = jnp.sum(jnp.where(ids[:, None] < ids[None, :], chips[:, None], 0), axis=0)
    here = yl * 32 + jnp.arange(32, dtype=jnp.int32)
    expert = jnp.sum((start[None, :] <= here[:, None]).astype(jnp.int32), axis=1) - 1
    index = ((expert >> 3) ^ yl) * 8 + (((expert >> 2) & 1) ^ core) * 4 + (expert & 3)

    send, dest = dispatch(targets, slot_expert, route_weight, tokens, cotangent)
    got = lax.all_to_all(
        send.reshape(CHIPS, UNITS, 2 * D), CHIP_AXES, split_axis=0, concat_axis=0, tiled=True
    ).reshape(ROWS, 2 * D)
    x, dy = got[:, :D], got[:, D:]

    def spread(v):
        return lax.all_to_all(v, DEV_AXES, split_axis=0, concat_axis=0, tiled=True)

    own_in = spread(select_rows(index, near[0], far[0])).reshape(D, HALF)
    own_out = spread(select_rows(index, near[1], far[1])).reshape(FF, HALF)
    oth_in = over_core(own_in)
    oth_out = over_core(own_out)

    one, two = dot(x, own_in), dot(x, oth_in)
    gating = jnp.where(is0, one, two)
    upward = jnp.where(is0, two, one)
    logistic = jax.nn.sigmoid(gating)
    active = gating * logistic
    derivative = logistic * (1.0 + gating * (1.0 - logistic))
    hidden = (active * upward).astype(BF)

    dy_own, dy_oth = half_of(dy, core), half_of(dy, 1 - core)
    give_out = over_core(dot_tn(hidden, dy_oth).astype(BF))
    grad_out = (dot_tn(hidden, dy_own) + give_out.astype(F32)).astype(BF)
    rows_out = spread(grad_out.reshape(32, 32, HALF))

    dhidden = dot_nt(dy_own, own_out) + dot_nt(dy_oth, oth_out)
    d_gate = dhidden * upward * derivative
    d_up = dhidden * active
    d_own = jnp.where(is0, d_gate, d_up).astype(BF)
    d_oth = jnp.where(is0, d_up, d_gate).astype(BF)
    give_in = over_core(dot_tn(x, d_oth).astype(BF))
    grad_in = (dot_tn(x, d_own) + give_in.astype(F32)).astype(BF)
    rows_in = spread(grad_in.reshape(32, 64, HALF))

    res_own, res_oth = dot(hidden, own_out).astype(BF), dot(hidden, oth_out).astype(BF)
    rows_dx = (dot_nt(d_own, own_in) + dot_nt(d_oth, oth_in)).astype(BF)
    result = jnp.concatenate(
        [jnp.where(is0, res_own, res_oth), jnp.where(is0, res_oth, res_own), rows_dx], axis=1
    )
    back = lax.all_to_all(
        result.reshape(CHIPS, UNITS, 2 * D), CHIP_AXES, split_axis=0, concat_axis=0, tiled=True
    ).reshape(ROWS, 2 * D)
    mixed, token_grad, mix_grad = combine(dest, route_weight, cotangent, back)

    def collect(rows):
        part = sum_rows(index, rows)
        r = rows.shape[1]
        part = part.reshape(2, 2, 4, r, HALF)
        other = over_core(part[:, 1])
        ours = part[:, 0]
        come_ours, come_other = over_y(jnp.stack([ours[1], other[1]]))
        sum_ours = ours[0].astype(F32) + come_ours.astype(F32)
        sum_other = other[0].astype(F32) + come_other.astype(F32)
        return jnp.concatenate(
            [jnp.where(is0, sum_ours, sum_other), jnp.where(is0, sum_other, sum_ours)], axis=2
        )

    sum_out = collect(rows_out)
    sum_in = collect(rows_in)
    trained_in, mean_in, square_in = adam_step(proj_in, first_in, second_in, sum_in)
    trained_out, mean_out, square_out = adam_step(proj_out, first_out, second_out, sum_out)
    return (
        mixed,
        token_grad,
        mix_grad,
        trained_in,
        mean_in,
        square_in,
        trained_out,
        mean_out,
        square_out,
    )


def solution(mesh):
    fine = Mesh(mesh.devices.reshape(2, 2, 4, 4, 2), ALL_AXES)
    rows = P(ALL_AXES, None)
    state = P(("yl", "core"), DEV_AXES, None)
    in_specs = (rows, rows, rows, P(), rows) + (state,) * 6
    out_specs = (rows, rows, rows) + (state,) * 6
    return jax.shard_map(on_device, mesh=fine, in_specs=in_specs, out_specs=out_specs, check_vma=False)
```

```python
import jax
import jax.numpy as jnp
from jax import lax
from jax.experimental import pallas as pl
from jax.experimental.pallas import tpu as pltpu
from jax.sharding import Mesh, PartitionSpec as P

D = 2048
FF = 1024
E = 16
CAP = 3
UNITS = 8
CHIPS = 64
ROWS = CHIPS * UNITS
HALF = 1024
HERE = 32
FAR = 4

BF = jnp.bfloat16
F32 = jnp.float32

beta_first = 0.9
beta_second = 0.95
learn_rate = 0.01
decay_rate = 0.1
adam_eps = 1e-08
bias_first = 1.0 - 0.9**10
bias_second = 1.0 - 0.95**10

CHIP_AXES = ("yl", "x", "z", "yh")
DEV_AXES = ("x", "z", "yh")
SEND_AXES = ("yh", "x", "z")
ALL_AXES = ("yl", "core", "x", "z", "yh")


def params(mib=48):
    return pltpu.CompilerParams(vmem_limit_bytes=mib * 2**20)


SHORT = pl.CostEstimate(flops=1, bytes_accessed=1, transcendentals=0)
LONG = pl.CostEstimate(flops=10**10, bytes_accessed=2 * 10**7, transcendentals=0)


def adam_step(weight, moment, square, gradient):
    new_moment = beta_first * moment + (1.0 - beta_first) * gradient
    new_square = beta_second * square + (1.0 - beta_second) * gradient * gradient
    update = (
        new_moment / bias_first / (jnp.sqrt(new_square / bias_second) + adam_eps)
        + decay_rate * weight
    )
    return (weight - learn_rate * update, new_moment, new_square)


def down(mask, value=1.0):
    return jnp.sum(jnp.where(mask, value, 0.0), axis=0, keepdims=True)


def across(mask, value=1.0):
    return jnp.sum(jnp.where(mask, value, 0.0), axis=1, keepdims=True)


def grids():
    sub = lax.broadcasted_iota(jnp.int32, (128, 128), 0).astype(F32)
    lane = lax.broadcasted_iota(jnp.int32, (128, 128), 1).astype(F32)
    return sub, lane


def plan_kernel(ecol, erow, plan, slot_rows, slot_cols):
    sub, lane = grids()
    ec, er = ecol[...].astype(F32), erow[...].astype(F32)

    chips_r = jnp.floor((CAP * down(ec == lane) + (UNITS - 1)) / UNITS)
    chips_c = jnp.floor((CAP * across(er == sub) + (UNITS - 1)) / UNITS)
    expert = (sub < E) & (lane < E)
    low_s, low_l = sub < E // 2, lane < E // 2
    same = expert & (low_s == low_l)
    ahead_r = same & ((chips_c > chips_r) | ((chips_c == chips_r) & (sub < lane)))
    ahead_c = same & ((chips_r > chips_c) | ((chips_r == chips_c) & (lane < sub)))
    rank_r = down(ahead_r)
    over_r = jnp.maximum(down(same, chips_c) - HERE, 0.0)
    over_c = jnp.maximum(across(same, chips_r) - HERE, 0.0)
    spill_r = jnp.clip(over_r - down(ahead_r, chips_c), 0.0, chips_r)
    spill_c = jnp.clip(over_c - across(ahead_c, chips_r), 0.0, chips_c)
    keep_r, keep_c = chips_r - spill_r, chips_c - spill_c
    across_y = expert & (low_s != low_l)
    kept_r = down(same & (sub < lane), keep_c)
    kept_c = across(same & (lane < sub), keep_r)
    spilt_r = down(across_y, keep_c) + down(same & (sub < lane), spill_c)
    spilt_c = across(across_y, keep_r) + across(same & (lane < sub), spill_r)
    y_r = jnp.where(low_l[0:1, :], 0.0, 1.0 * HERE)
    y_c = jnp.where(low_s[:, 0:1], 0.0, 1.0 * HERE)
    kept_r, kept_c = kept_r + y_r, kept_c + y_c
    spilt_r, spilt_c = spilt_r + (HERE - y_r), spilt_c + (HERE - y_c)
    for i, v in enumerate((rank_r, keep_r, spill_r, kept_r, spilt_r)):
        plan[i : i + 1, :] = v.astype(jnp.int32)

    mine_c, mine_r = ec == lane, er == sub
    slot_cols[:, 0:1] = CAP * across((ec == er) & (lane < sub))
    slot_rows[0:1, :] = CAP * down((ec == er) & (sub < lane))
    for i, (r, c) in enumerate(((keep_r, keep_c), (kept_r, kept_c), (spilt_r - keep_r, spilt_c - keep_c))):
        slot_cols[:, i + 1 : i + 2] = UNITS * across(mine_c, r)
        slot_rows[i + 1 : i + 2, :] = UNITS * down(mine_r, c)


def make_plan(slot_expert):
    return pl.pallas_call(
        plan_kernel,
        out_shape=(
            jax.ShapeDtypeStruct((8, 128), jnp.int32),
            jax.ShapeDtypeStruct((8, 128), F32),
            jax.ShapeDtypeStruct((128, 8), F32),
        ),
        compiler_params=params(),
        name="plan",
    )(slot_expert.reshape(128, 1), slot_expert.reshape(1, 128))


def dispatch_kernel(tcol, trow, slot_rows, slot_cols, wrow, tok, cot, send, dest):
    sub, lane = grids()
    tc = [tcol[:, k : k + 1].astype(F32) for k in range(2)]
    tr = [trow[k : k + 1, :].astype(F32) for k in range(2)]
    dest_row = []
    for k in range(2):
        at = sub == tr[k]
        pos = down((tc[0] == tr[k]) & (sub < lane)) + down((tc[1] == tr[k]) & (sub < lane))
        slot, limit, first, rest = (down(at, slot_cols[:, i : i + 1]) for i in range(4))
        unit = slot + pos
        row = unit + jnp.where(unit < limit, first, rest)
        dest_row.append(jnp.where(pos < CAP, row, 4.0 * ROWS))
        at = lane == tc[k]
        pos = across((tc[k] == tr[0]) & (lane < sub)) + across((tc[k] == tr[1]) & (lane < sub))
        slot, limit, first, rest = (across(at, slot_rows[i : i + 1, :]) for i in range(4))
        unit = slot + pos
        row = unit + jnp.where(unit < limit, first, rest)
        dest[:, k : k + 1] = jnp.where(pos < CAP, row, 4.0 * ROWS)

    w0, w1 = wrow[0:1, :], wrow[1:2, :]
    for part in range(ROWS // 128):
        place = sub + 128.0 * part
        first, second = place == dest_row[0], place == dest_row[1]
        pick = jnp.where(first | second, 1.0, 0.0).astype(BF)
        weight = across(first, w0) + across(second, w1)
        rows = slice(part * 128, part * 128 + 128)
        send[rows, :D] = jnp.dot(pick, tok[...], preferred_element_type=F32).astype(BF)
        send[rows, D:] = (jnp.dot(pick, cot[...], preferred_element_type=F32) * weight).astype(BF)


def dispatch(targets, slot_rows, slot_cols, route_weight, tokens, cotangent):
    return pl.pallas_call(
        dispatch_kernel,
        out_shape=(
            jax.ShapeDtypeStruct((ROWS, 2 * D), BF),
            jax.ShapeDtypeStruct((128, 2), F32),
        ),
        compiler_params=params(),
        name="dispatch",
    )(targets, targets.T, slot_rows, slot_cols, route_weight.T, tokens, cotangent)


def combine_kernel(dest, weight, cot, back, mixed, grad, mix):
    place = lax.broadcasted_iota(jnp.int32, (128, ROWS), 1).astype(F32)
    first, second = place == dest[:, 0:1], place == dest[:, 1:2]
    one, zero = jnp.float32(1.0), jnp.float32(0.0)
    pick0 = jnp.where(first, one, zero).astype(BF)
    pick1 = jnp.where(second, one, zero).astype(BF)
    both = jnp.where(first | second, one, zero).astype(BF)
    w0, w1 = weight[:, 0:1], weight[:, 1:2]
    mix0 = jnp.zeros((128, 1), F32)
    mix1 = jnp.zeros((128, 1), F32)
    width = 512
    for c in range(D // width):
        cols = slice(c * width, (c + 1) * width)
        out0 = jnp.dot(pick0, back[:, cols], preferred_element_type=F32)
        out1 = jnp.dot(pick1, back[:, cols], preferred_element_type=F32)
        here = cot[:, cols].astype(F32)
        mixed[:, cols] = (w0 * out0 + w1 * out1).astype(BF)
        mix0 += jnp.sum(here * out0, axis=1, keepdims=True)
        mix1 += jnp.sum(here * out1, axis=1, keepdims=True)
        dcols = slice(D + c * width, D + (c + 1) * width)
        grad[:, cols] = jnp.dot(both, back[:, dcols], preferred_element_type=F32).astype(BF)
    mix[:, 0:1] = mix0
    mix[:, 1:2] = mix1


def combine(dest, route_weight, cotangent, back):
    return pl.pallas_call(
        combine_kernel,
        out_shape=(
            jax.ShapeDtypeStruct((128, D), BF),
            jax.ShapeDtypeStruct((128, D), BF),
            jax.ShapeDtypeStruct((128, 2), F32),
        ),
        compiler_params=params(),
        name="combine",
    )(dest, route_weight, cotangent, back)


def prepare_kernel(core, w_in, w_out, mine, theirs):
    left_in, right_in = w_in[:, :, :HALF].astype(BF), w_in[:, :, HALF:].astype(BF)
    left_out, right_out = w_out[:, :, :HALF].astype(BF), w_out[:, :, HALF:].astype(BF)

    def put(left, right):
        left[:, :64], right[:, :64] = left_in, right_in
        left[:, 64:], right[:, 64:] = left_out, right_out

    @pl.when(core[0] == 0)
    def _():
        put(mine, theirs)

    @pl.when(core[0] != 0)
    def _():
        put(theirs, mine)


def prepare(core, w_in, w_out):
    n, r, c = w_in.shape
    ro = w_out.shape[1]
    half = pl.BlockSpec((1, r + ro, HALF), lambda i, s: (i, 0, 0))
    return pl.pallas_call(
        prepare_kernel,
        grid_spec=pltpu.PrefetchScalarGridSpec(
            num_scalar_prefetch=1,
            grid=(n,),
            in_specs=[
                pl.BlockSpec((1, r, c), lambda i, s: (i, 0, 0)),
                pl.BlockSpec((1, ro, c), lambda i, s: (i, 0, 0)),
            ],
            out_specs=[half, half],
        ),
        out_shape=[jax.ShapeDtypeStruct((n, r + ro, HALF), BF)] * 2,
        compiler_params=params(),
        name="prepare",
    )(core, w_in, w_out)


def copy_one(e, parts, out, j):
    for k, part in enumerate(parts):

        @pl.when((e >= 4 * k) & (e < 4 * k + 4))
        def _(k=k, part=part):
            out[j] = part[jnp.clip(e - 4 * k, 0, 3)]


def take_kernel(index, mine, theirs, out):
    for j in range(FAR):
        copy_one(index[j], (mine, theirs), out, j)


def take_rows(index, mine, theirs):
    n, r, c = mine.shape
    whole = pl.BlockSpec((n, r, c), lambda i, s: (0, 0, 0))
    return pl.pallas_call(
        take_kernel,
        grid_spec=pltpu.PrefetchScalarGridSpec(
            num_scalar_prefetch=1, grid=(1,), in_specs=[whole] * 2, out_specs=whole
        ),
        out_shape=jax.ShapeDtypeStruct((FAR, r, c), BF),
        compiler_params=params(),
        name="take_rows",
    )(index, mine, theirs)


def select_kernel(index, mine, theirs, far, out):
    step = pl.program_id(0)
    for j in range(8):
        copy_one(index[step * 8 + j], (mine, theirs, far), out, j)


def select_rows(index, mine, theirs, far, start, r):
    c = mine.shape[2]
    part = pl.BlockSpec((4, r, c), lambda i, s: (0, start // r, 0))
    return pl.pallas_call(
        select_kernel,
        grid_spec=pltpu.PrefetchScalarGridSpec(
            num_scalar_prefetch=1,
            grid=(4,),
            in_specs=[part] * 3,
            out_specs=pl.BlockSpec((8, r, c), lambda i, s: (i, 0, 0)),
        ),
        out_shape=jax.ShapeDtypeStruct((32, r, c), BF),
        compiler_params=params(),
        name="select_rows",
    )(index, mine, theirs, far)


def sum_kernel(index, rows, mine, theirs, far, total):
    total[...] = jnp.zeros_like(total)
    for d in range(32):
        e = index[d]
        total[e] += rows[d].astype(F32)
    mine[...] = total[:4].astype(BF)
    theirs[...] = total[4:8].astype(BF)
    far[...] = total[8:].astype(BF)


def sum_rows(index, rows):
    n, r, c = rows.shape
    step = 16
    return pl.pallas_call(
        sum_kernel,
        grid_spec=pltpu.PrefetchScalarGridSpec(
            num_scalar_prefetch=1,
            grid=(r // step,),
            in_specs=[pl.BlockSpec((n, step, c), lambda i, s: (0, i, 0))],
            out_specs=[pl.BlockSpec((4, step, c), lambda i, s: (0, i, 0))] * 3,
            scratch_shapes=[pltpu.VMEM((8 + FAR, step, c), F32)],
        ),
        out_shape=[jax.ShapeDtypeStruct((4, r, c), BF)] * 3,
        compiler_params=params(),
        cost_estimate=LONG,
        name="sum_rows",
    )(index, rows)


def adam_kernel(sel, weight, moment, square, near0, near1, far0, far1, new_w, new_m, new_s):
    has_far = (sel[1 + pl.program_id(0)] < FAR).astype(F32)
    for h in range(2):
        cols = slice(h * HALF, (h + 1) * HALF)
        own = sel[0] == h
        near = jnp.where(own, near0[...], near1[...]).astype(F32)
        far = jnp.where(own, far0[...], far1[...]).astype(F32)
        new_w[:, :, cols], new_m[:, :, cols], new_s[:, :, cols] = adam_step(
            weight[:, :, cols], moment[:, :, cols], square[:, :, cols], near + has_far * far
        )


def adam(sel, weight, moment, square, near0, near1, far0, far1):
    n, r, c = weight.shape
    state = pl.BlockSpec((1, r, c), lambda i, s: (i, 0, 0))
    near = pl.BlockSpec((1, r, HALF), lambda i, s: (i, 0, 0))
    far = pl.BlockSpec((1, r, HALF), lambda i, s: (jnp.minimum(s[1 + i], FAR - 1), 0, 0))
    return pl.pallas_call(
        adam_kernel,
        grid_spec=pltpu.PrefetchScalarGridSpec(
            num_scalar_prefetch=1,
            grid=(n,),
            in_specs=[state] * 3 + [near] * 2 + [far] * 2,
            out_specs=[state] * 3,
        ),
        out_shape=[jax.ShapeDtypeStruct((n, r, c), F32)] * 3,
        compiler_params=params(),
        cost_estimate=LONG,
        name="adam",
    )(sel, weight, moment, square, near0, near1, far0, far1)


def rows_of(w):
    return jnp.concatenate([w[y, i] for i in range(w.shape[1]) for y in range(2)], axis=0)


def put_rows(out, v):
    r = out.shape[2]
    for i in range(out.shape[1]):
        for y in range(2):
            out[y, i] = v[(2 * i + y) * r : (2 * i + y + 1) * r].astype(BF)


def call(kernel, core, args, in_specs, out_shape, out_specs, steps, name, cost=SHORT):
    return pl.pallas_call(
        kernel,
        grid_spec=pltpu.PrefetchScalarGridSpec(
            num_scalar_prefetch=1, grid=(steps,), in_specs=in_specs, out_specs=out_specs
        ),
        out_shape=out_shape,
        compiler_params=params(56),
        cost_estimate=cost,
        name=name,
    )(core, *args)


def hidden_kernel(core, x, own, oth, hidden, hidden_t, active, steep):
    one, two = dot(x[...], rows_of(own)), dot(x[...], rows_of(oth))
    is0 = core[0] == 0
    gating, upward = jnp.where(is0, one, two), jnp.where(is0, two, one)
    logistic = jax.nn.sigmoid(gating)
    act = gating * logistic
    hid = act * upward
    hidden[...] = hid.astype(BF)
    hidden_t[...] = hid.T.astype(BF)
    active[...] = act
    steep[...] = upward * (logistic * (1.0 + gating * (1.0 - logistic)))


def other_hidden_kernel(core, x, own, oth, hidden_t):
    one, two = dot(x[...], rows_of(own)), dot(x[...], rows_of(oth))
    is0 = core[0] == 0
    gating, upward = jnp.where(is0, one, two), jnp.where(is0, two, one)
    hidden_t[...] = (gating * jax.nn.sigmoid(gating) * upward).T.astype(BF)


def other_hidden_of(core, got, own, oth):
    w = pl.BlockSpec((2, 16, 64, 256), lambda j, s: (0, 0, 0, j))
    return call(
        other_hidden_kernel,
        core,
        (got, own, oth),
        [pl.BlockSpec((ROWS, D), lambda j, s: (0, 0)), w, w],
        jax.ShapeDtypeStruct((FF, ROWS), BF),
        pl.BlockSpec((256, ROWS), lambda j, s: (j, 0)),
        FF // 256,
        "other_hidden",
    )


def hidden_of(core, got, own, oth):
    w = pl.BlockSpec((2, 16, 64, 256), lambda j, s: (0, 0, 0, j))
    tile = pl.BlockSpec((ROWS, 256), lambda j, s: (0, j))
    return call(
        hidden_kernel,
        core,
        (got, own, oth),
        [pl.BlockSpec((ROWS, D), lambda j, s: (0, 0)), w, w],
        [
            jax.ShapeDtypeStruct((ROWS, FF), BF),
            jax.ShapeDtypeStruct((FF, ROWS), BF),
            jax.ShapeDtypeStruct((ROWS, FF), F32),
            jax.ShapeDtypeStruct((ROWS, FF), F32),
        ],
        [tile, pl.BlockSpec((256, ROWS), lambda j, s: (j, 0)), tile, tile],
        FF // 256,
        "hidden",
    )


def outer_kernel(core, a_t, a2_t, b, b2, out):
    put_rows(out, dot(a_t[...], b[...]) + dot(a2_t[...], b2[...]))


def outer(core, a_t, a2_t, b, b2, place, name):
    m, k = a_t.shape
    left = pl.BlockSpec((m, k), lambda j, s: (0, 0))
    right = pl.BlockSpec((k, 256), lambda j, s: (0, 4 * place(s[0]) + j))
    return call(
        outer_kernel,
        core,
        (a_t, a2_t, b, b2),
        [left, left, right, right],
        jax.ShapeDtypeStruct((2, 16, m // 32, HALF), BF),
        pl.BlockSpec((2, 16, m // 32, 256), lambda j, s: (0, 0, 0, j)),
        4,
        name,
    )


def flip_kernel(core, one, two, one_t, two_t):
    one_t[...] = one[...].T
    two_t[...] = two[...].T


def flip(core, one, two):
    rows = pl.BlockSpec((ROWS, 512), lambda j, s: (0, j))
    return call(
        flip_kernel,
        core,
        (one, two),
        [rows, rows],
        [jax.ShapeDtypeStruct((D, ROWS), BF)] * 2,
        [pl.BlockSpec((512, ROWS), lambda j, s: (j, 0))] * 2,
        4,
        "flip",
        LONG,
    )


def back_kernel(core, dy_own, dy_oth, own, oth, active, steep, d_own, d_oth):
    dhidden = dot_nt(dy_own[...], rows_of(own)) + dot_nt(dy_oth[...], rows_of(oth))
    d_gate = (dhidden * steep[...]).astype(BF)
    d_up = (dhidden * active[...]).astype(BF)
    is0 = core[0] == 0
    d_own[...] = jnp.where(is0, d_gate, d_up)
    d_oth[...] = jnp.where(is0, d_up, d_gate)


def back_of(core, got, own, oth, active, steep):
    w = pl.BlockSpec((2, 4, 32, HALF), lambda j, s: (0, j, 0, 0))
    tile = pl.BlockSpec((ROWS, 256), lambda j, s: (0, j))
    return call(
        back_kernel,
        core,
        (got, got, own, oth, active, steep),
        [
            pl.BlockSpec((ROWS, HALF), lambda j, s: (0, 2 + s[0])),
            pl.BlockSpec((ROWS, HALF), lambda j, s: (0, 3 - s[0])),
            w,
            w,
            tile,
            tile,
        ],
        [jax.ShapeDtypeStruct((ROWS, FF), BF)] * 2,
        [tile, tile],
        FF // 256,
        "back",
    )


def give_kernel(core, hidden, d_own, d_oth, own_out, oth_out, own_in, oth_in, out):
    step = pl.program_id(0)

    @pl.when(step == 0)
    def _():
        out[...] = dot(hidden[...], rows_of(own_out)).astype(BF)

    @pl.when(step == 1)
    def _():
        out[...] = dot(hidden[...], rows_of(oth_out)).astype(BF)

    @pl.when(step >= 2)
    def _():
        dx = dot_nt(d_own[...], rows_of(own_in)) + dot_nt(d_oth[...], rows_of(oth_in))
        out[...] = dx.astype(BF)


def give_of(core, hidden, d_own, d_oth, own_out, oth_out, own_in, oth_in):
    row = pl.BlockSpec((ROWS, FF), lambda j, s: (0, 0))
    w_out = pl.BlockSpec((2, 16, 32, HALF), lambda j, s: (0, 0, 0, 0))
    w_in = pl.BlockSpec((2, 8, 64, HALF), lambda j, s: (0, jnp.maximum(j - 2, 0), 0, 0))
    return call(
        give_kernel,
        core,
        (hidden, d_own, d_oth, own_out, oth_out, own_in, oth_in),
        [row, row, row, w_out, w_out, w_in, w_in],
        jax.ShapeDtypeStruct((ROWS, 2 * D), BF),
        pl.BlockSpec(
            (ROWS, HALF), lambda j, s: (0, jnp.where(j == 0, s[0], jnp.where(j == 1, 1 - s[0], j)))
        ),
        4,
        "give",
        LONG,
    )


def dot(a, b):
    return jnp.dot(a, b, preferred_element_type=F32)


def dot_nt(a, b):
    return lax.dot_general(a, b, (((1,), (1,)), ((), ())), preferred_element_type=F32)


def dot_tn(a, b):
    return lax.dot_general(a, b, (((0,), (0,)), ((), ())), preferred_element_type=F32)


def over_core(v):
    return lax.ppermute(v, "core", [(0, 1), (1, 0)])


def over_y(v):
    return lax.ppermute(v, "yl", [(0, 1), (1, 0)])


def on_device(
    tokens,
    cotangent,
    route_weight,
    slot_expert,
    targets,
    proj_in,
    first_in,
    second_in,
    proj_out,
    first_out,
    second_out,
):
    core = lax.axis_index("core")
    yl = lax.axis_index("yl")
    which = core[None].astype(jnp.int32)

    def after(v, *first):
        return lax.optimization_barrier((v, *first))[0]

    def spread(v):
        got = lax.all_to_all(v.reshape(32, *v.shape[-2:]), SEND_AXES, split_axis=0, concat_axis=0, tiled=True)
        return got.reshape(2, 16, *v.shape[-2:])

    def exchange(v):
        return lax.all_to_all(
            v.reshape(CHIPS, UNITS, 2 * D), CHIP_AXES, split_axis=0, concat_axis=0, tiled=True
        ).reshape(ROWS, 2 * D)

    plan, slot_rows, slot_cols = make_plan(slot_expert)

    rank, keep, spill, kept, spilt = (plan[i, :E] for i in range(5))
    ids = jnp.arange(E, dtype=jnp.int32)
    stored = (ids >> 3) == yl
    place = jnp.where(stored, (((ids >> 2) & 1) ^ core) * 4 + (ids & 3), 8 + rank)
    begin = jnp.where(stored, kept, spilt)
    length = jnp.where(stored, keep, spill)
    order = jnp.arange(HERE, dtype=jnp.int32)
    here = yl * HERE + ((order & 15) * 2 + (order >> 4))[:, None]
    index = jnp.sum(jnp.where((begin <= here) & (here < begin + length), place, 0), axis=1)
    ranked = stored & (rank == jnp.arange(FAR, dtype=jnp.int32)[:, None])
    largest = jnp.sum(jnp.where(ranked, place, 0), axis=1)
    own_rank = lax.dynamic_slice_in_dim(rank, (yl * 2 + core) * 4, 4)
    sel = jnp.concatenate([which, own_rank])

    mine, theirs = prepare(which, proj_in, proj_out)
    theirs = over_core(theirs)
    taken = take_rows(largest, mine, theirs)
    far = over_y(taken)
    send, dest = dispatch(targets, slot_rows, slot_cols, route_weight, after(tokens, taken), cotangent)
    got = exchange(after(send, far))
    for_in = select_rows(index, mine, theirs, far, 0, 64)
    for_out = select_rows(index, mine, theirs, far, 64, 32)
    for_in, for_out, got = lax.optimization_barrier((for_in, for_out, got))
    got2 = over_core(got)
    x_t, x2_t = flip(which, got, got2)
    own_in = spread(for_in)
    oth_in = over_core(own_in)
    own_out = spread(after(for_out, own_in))

    hidden, hidden_t, active, steep = hidden_of(which, got, own_in, oth_in)
    hidden2_t = other_hidden_of(which, got2, own_in, oth_in)
    grad_out = outer(which, hidden_t, hidden2_t, got, got2, lambda c: 2 + c, "outer_out")
    grad_out, own_out = lax.optimization_barrier((grad_out, own_out))
    oth_out = over_core(own_out)
    rows_out = spread(grad_out)

    d_own, d_oth = back_of(which, got, own_out, oth_out, after(active, grad_out), steep)
    d2_own = over_core(d_oth)
    grad_in = outer(which, x_t, x2_t, d_own, d2_own, lambda c: 0, "outer_in")
    rows_in = spread(after(grad_in, rows_out))

    def gather_sums(rows):
        near, near_other, spilled = sum_rows(index, rows.reshape(32, *rows.shape[2:]))
        return near, over_core(near_other), over_y(spilled)

    near0, near1, far_out = gather_sums(rows_out)
    trained_out, mean_out, square_out = adam(
        sel, proj_out, first_out, second_out, near0, near1, far_out, over_core(far_out)
    )
    result = give_of(which, hidden, d_own, d_oth, own_out, oth_out, own_in, oth_in)
    near0, near1, far_in = gather_sums(rows_in)
    back = exchange(after(result, far_in, far_out))
    trained_in, mean_in, square_in = adam(
        sel, proj_in, first_in, second_in, near0, near1, far_in, over_core(far_in)
    )
    mixed, token_grad, mix_grad = combine(dest, route_weight, cotangent, back)
    return (
        mixed,
        token_grad,
        mix_grad,
        trained_in,
        mean_in,
        square_in,
        trained_out,
        mean_out,
        square_out,
    )


def solution(mesh):
    fine = Mesh(mesh.devices.reshape(2, 2, 4, 4, 2), ALL_AXES)
    rows = P(ALL_AXES, None)
    state = P(("yl", "core"), DEV_AXES, None)
    in_specs = (rows, rows, rows, P(), rows) + (state,) * 6
    out_specs = (rows, rows, rows) + (state,) * 6
    return jax.shard_map(on_device, mesh=fine, in_specs=in_specs, out_specs=out_specs, check_vma=False)
```

```python
import jax
import jax.numpy as jnp
from jax import lax
from jax.experimental import pallas as pl
from jax.experimental.pallas import tpu as pltpu
from jax.sharding import Mesh, PartitionSpec as P

D = 2048
FF = 1024
E = 16
CAP = 3
UNITS = 8
CHIPS = 64
ROWS = CHIPS * UNITS
HALF = 1024
HERE = 32
FAR = 4

BF = jnp.bfloat16
F32 = jnp.float32

beta_first = 0.9
beta_second = 0.95
learn_rate = 0.01
decay_rate = 0.1
adam_eps = 1e-08
bias_first = 1.0 - 0.9**10
bias_second = 1.0 - 0.95**10

CHIP_AXES = ("yl", "x", "z", "yh")
DEV_AXES = ("x", "z", "yh")
SEND_AXES = ("yh", "x", "z")
ALL_AXES = ("yl", "core", "x", "z", "yh")


def params(mib=48):
    return pltpu.CompilerParams(vmem_limit_bytes=mib * 2**20)


SHORT = pl.CostEstimate(flops=1, bytes_accessed=1, transcendentals=0)
LONG = pl.CostEstimate(flops=10**10, bytes_accessed=2 * 10**7, transcendentals=0)


def adam_step(weight, moment, square, gradient):
    new_moment = beta_first * moment + (1.0 - beta_first) * gradient
    new_square = beta_second * square + (1.0 - beta_second) * gradient * gradient
    update = (
        new_moment / bias_first / (jnp.sqrt(new_square / bias_second) + adam_eps)
        + decay_rate * weight
    )
    return (weight - learn_rate * update, new_moment, new_square)


def down(mask, value=1.0):
    return jnp.sum(jnp.where(mask, value, 0.0), axis=0, keepdims=True)


def across(mask, value=1.0):
    return jnp.sum(jnp.where(mask, value, 0.0), axis=1, keepdims=True)


def grids():
    sub = lax.broadcasted_iota(jnp.int32, (128, 128), 0).astype(F32)
    lane = lax.broadcasted_iota(jnp.int32, (128, 128), 1).astype(F32)
    return sub, lane


def plan_kernel(ecol, erow, plan, slot_rows, slot_cols):
    sub, lane = grids()
    ec, er = ecol[...].astype(F32), erow[...].astype(F32)

    chips_r = jnp.floor((CAP * down(ec == lane) + (UNITS - 1)) / UNITS)
    chips_c = jnp.floor((CAP * across(er == sub) + (UNITS - 1)) / UNITS)
    expert = (sub < E) & (lane < E)
    low_s, low_l = sub < E // 2, lane < E // 2
    same = expert & (low_s == low_l)
    ahead_r = same & ((chips_c > chips_r) | ((chips_c == chips_r) & (sub < lane)))
    ahead_c = same & ((chips_r > chips_c) | ((chips_r == chips_c) & (lane < sub)))
    rank_r = down(ahead_r)
    over_r = jnp.maximum(down(same, chips_c) - HERE, 0.0)
    over_c = jnp.maximum(across(same, chips_r) - HERE, 0.0)
    spill_r = jnp.clip(over_r - down(ahead_r, chips_c), 0.0, chips_r)
    spill_c = jnp.clip(over_c - across(ahead_c, chips_r), 0.0, chips_c)
    keep_r, keep_c = chips_r - spill_r, chips_c - spill_c
    across_y = expert & (low_s != low_l)
    kept_r = down(same & (sub < lane), keep_c)
    kept_c = across(same & (lane < sub), keep_r)
    spilt_r = down(across_y, keep_c) + down(same & (sub < lane), spill_c)
    spilt_c = across(across_y, keep_r) + across(same & (lane < sub), spill_r)
    y_r = jnp.where(low_l[0:1, :], 0.0, 1.0 * HERE)
    y_c = jnp.where(low_s[:, 0:1], 0.0, 1.0 * HERE)
    kept_r, kept_c = kept_r + y_r, kept_c + y_c
    spilt_r, spilt_c = spilt_r + (HERE - y_r), spilt_c + (HERE - y_c)
    for i, v in enumerate((rank_r, keep_r, spill_r, kept_r, spilt_r)):
        plan[i : i + 1, :] = v.astype(jnp.int32)

    mine_c, mine_r = ec == lane, er == sub
    slot_cols[:, 0:1] = CAP * across((ec == er) & (lane < sub))
    slot_rows[0:1, :] = CAP * down((ec == er) & (sub < lane))
    for i, (r, c) in enumerate(((keep_r, keep_c), (kept_r, kept_c), (spilt_r - keep_r, spilt_c - keep_c))):
        slot_cols[:, i + 1 : i + 2] = UNITS * across(mine_c, r)
        slot_rows[i + 1 : i + 2, :] = UNITS * down(mine_r, c)


def make_plan(slot_expert):
    return pl.pallas_call(
        plan_kernel,
        out_shape=(
            jax.ShapeDtypeStruct((8, 128), jnp.int32),
            jax.ShapeDtypeStruct((8, 128), F32),
            jax.ShapeDtypeStruct((128, 8), F32),
        ),
        compiler_params=params(),
        name="plan",
    )(slot_expert.reshape(128, 1), slot_expert.reshape(1, 128))


def dispatch_kernel(tcol, trow, slot_rows, slot_cols, wrow, tok, cot, send, dest):
    sub, lane = grids()
    tc = [tcol[:, k : k + 1].astype(F32) for k in range(2)]
    tr = [trow[k : k + 1, :].astype(F32) for k in range(2)]
    dest_row = []
    for k in range(2):
        at = sub == tr[k]
        pos = down((tc[0] == tr[k]) & (sub < lane)) + down((tc[1] == tr[k]) & (sub < lane))
        slot, limit, first, rest = (down(at, slot_cols[:, i : i + 1]) for i in range(4))
        unit = slot + pos
        row = unit + jnp.where(unit < limit, first, rest)
        dest_row.append(jnp.where(pos < CAP, row, 4.0 * ROWS))
        at = lane == tc[k]
        pos = across((tc[k] == tr[0]) & (lane < sub)) + across((tc[k] == tr[1]) & (lane < sub))
        slot, limit, first, rest = (across(at, slot_rows[i : i + 1, :]) for i in range(4))
        unit = slot + pos
        row = unit + jnp.where(unit < limit, first, rest)
        dest[:, k : k + 1] = jnp.where(pos < CAP, row, 4.0 * ROWS)

    w0, w1 = wrow[0:1, :], wrow[1:2, :]
    for part in range(ROWS // 128):
        place = sub + 128.0 * part
        first, second = place == dest_row[0], place == dest_row[1]
        pick = jnp.where(first | second, 1.0, 0.0).astype(BF)
        weight = across(first, w0) + across(second, w1)
        rows = slice(part * 128, part * 128 + 128)
        send[rows, :D] = jnp.dot(pick, tok[...], preferred_element_type=F32).astype(BF)
        send[rows, D:] = (jnp.dot(pick, cot[...], preferred_element_type=F32) * weight).astype(BF)


def dispatch(targets, slot_rows, slot_cols, route_weight, tokens, cotangent):
    return pl.pallas_call(
        dispatch_kernel,
        out_shape=(
            jax.ShapeDtypeStruct((ROWS, 2 * D), BF),
            jax.ShapeDtypeStruct((128, 2), F32),
        ),
        compiler_params=params(),
        name="dispatch",
    )(targets, targets.T, slot_rows, slot_cols, route_weight.T, tokens, cotangent)


def combine_kernel(dest, weight, cot, out, dx, mixed, grad, mix):
    step = pl.program_id(0)
    place = lax.broadcasted_iota(jnp.int32, (128, ROWS), 1).astype(F32)
    first, second = place == dest[:, 0:1], place == dest[:, 1:2]
    pick0 = jnp.where(first, 1.0, 0.0).astype(BF)
    pick1 = jnp.where(second, 1.0, 0.0).astype(BF)
    both = jnp.where(first | second, 1.0, 0.0).astype(BF)
    out0, out1 = dot(pick0, out[...]), dot(pick1, out[...])
    here = cot[...].astype(F32)
    mixed[...] = (weight[:, 0:1] * out0 + weight[:, 1:2] * out1).astype(BF)
    grad[...] = dot(both, dx[...]).astype(BF)

    @pl.when(step == 0)
    def _():
        mix[...] = jnp.zeros_like(mix)

    mix[:, 0:1] += jnp.sum(here * out0, axis=1, keepdims=True)
    mix[:, 1:2] += jnp.sum(here * out1, axis=1, keepdims=True)


def combine(dest, route_weight, cotangent, back):
    width = 512
    whole = pl.BlockSpec((128, 2), lambda j: (0, 0))
    tile = pl.BlockSpec((128, width), lambda j: (0, j))
    return pl.pallas_call(
        combine_kernel,
        grid=(D // width,),
        in_specs=[
            whole,
            whole,
            tile,
            pl.BlockSpec((ROWS, width), lambda j: (0, j)),
            pl.BlockSpec((ROWS, width), lambda j: (0, D // width + j)),
        ],
        out_specs=[tile, tile, whole],
        out_shape=(
            jax.ShapeDtypeStruct((128, D), BF),
            jax.ShapeDtypeStruct((128, D), BF),
            jax.ShapeDtypeStruct((128, 2), F32),
        ),
        compiler_params=params(),
        name="combine",
    )(dest, route_weight, cotangent, back, back)


def prepare_kernel(core, w_in, w_out, mine, theirs):
    left_in, right_in = w_in[:, :, :HALF].astype(BF), w_in[:, :, HALF:].astype(BF)
    left_out, right_out = w_out[:, :, :HALF].astype(BF), w_out[:, :, HALF:].astype(BF)

    def put(left, right):
        left[:, :64], right[:, :64] = left_in, right_in
        left[:, 64:], right[:, 64:] = left_out, right_out

    @pl.when(core[0] == 0)
    def _():
        put(mine, theirs)

    @pl.when(core[0] != 0)
    def _():
        put(theirs, mine)


def prepare(core, w_in, w_out):
    n, r, c = w_in.shape
    ro = w_out.shape[1]
    half = pl.BlockSpec((1, r + ro, HALF), lambda i, s: (i, 0, 0))
    return pl.pallas_call(
        prepare_kernel,
        grid_spec=pltpu.PrefetchScalarGridSpec(
            num_scalar_prefetch=1,
            grid=(n,),
            in_specs=[
                pl.BlockSpec((1, r, c), lambda i, s: (i, 0, 0)),
                pl.BlockSpec((1, ro, c), lambda i, s: (i, 0, 0)),
            ],
            out_specs=[half, half],
        ),
        out_shape=[jax.ShapeDtypeStruct((n, r + ro, HALF), BF)] * 2,
        compiler_params=params(),
        name="prepare",
    )(core, w_in, w_out)


def copy_one(e, parts, out, j):
    start = 0
    for part in parts:
        n = part.shape[0]

        @pl.when((e >= start) & (e < start + n))
        def _(start=start, n=n, part=part):
            out[j] = part[jnp.clip(e - start, 0, n - 1)]

        start += n


def take_kernel(index, mine, theirs, pair, cross):
    for j in range(FAR):
        copy_one(index[j], (mine, theirs), (pair, cross)[j // 2], j % 2)


def take_rows(index, mine, theirs):
    n, r, c = mine.shape
    whole = pl.BlockSpec((n, r, c), lambda i, s: (0, 0, 0))
    two = pl.BlockSpec((2, r, c), lambda i, s: (0, 0, 0))
    return pl.pallas_call(
        take_kernel,
        grid_spec=pltpu.PrefetchScalarGridSpec(
            num_scalar_prefetch=1, grid=(1,), in_specs=[whole] * 2, out_specs=[two] * 2
        ),
        out_shape=[jax.ShapeDtypeStruct((2, r, c), BF)] * 2,
        compiler_params=params(),
        name="take_rows",
    )(index, mine, theirs)


def select_kernel(index, *refs):
    step = pl.program_id(0)
    for j in range(8):
        copy_one(index[step * 8 + j], refs[:-1], refs[-1], j)


def select_rows(index, parts, start, r):
    c = parts[0].shape[2]
    return pl.pallas_call(
        select_kernel,
        grid_spec=pltpu.PrefetchScalarGridSpec(
            num_scalar_prefetch=1,
            grid=(4,),
            in_specs=[pl.BlockSpec((p.shape[0], r, c), lambda i, s: (0, start // r, 0)) for p in parts],
            out_specs=pl.BlockSpec((8, r, c), lambda i, s: (i, 0, 0)),
        ),
        out_shape=jax.ShapeDtypeStruct((32, r, c), BF),
        compiler_params=params(),
        name="select_rows",
    )(index, *parts)


def sum_kernel(index, rows, mine, theirs, pair, cross, total):
    total[...] = jnp.zeros_like(total)
    for d in range(32):
        e = index[d]
        total[e] += rows[d].astype(F32)
    mine[...] = total[:4].astype(BF)
    theirs[...] = total[4:8].astype(BF)
    pair[...] = total[8:10].astype(BF)
    cross[...] = total[10:].astype(BF)


def sum_rows(index, rows):
    n, r, c = rows.shape
    step = 16
    counts = (4, 4, 2, 2)
    return pl.pallas_call(
        sum_kernel,
        grid_spec=pltpu.PrefetchScalarGridSpec(
            num_scalar_prefetch=1,
            grid=(r // step,),
            in_specs=[pl.BlockSpec((n, step, c), lambda i, s: (0, i, 0))],
            out_specs=[pl.BlockSpec((k, step, c), lambda i, s: (0, i, 0)) for k in counts],
            scratch_shapes=[pltpu.VMEM((8 + FAR, step, c), F32)],
        ),
        out_shape=[jax.ShapeDtypeStruct((k, r, c), BF) for k in counts],
        compiler_params=params(),
        cost_estimate=LONG,
        name="sum_rows",
    )(index, rows)


def adam_kernel(sel, weight, moment, square, *refs):
    own, other = refs[:3], refs[3:6]
    new_w, new_m, new_s = refs[6:]
    rank = sel[1 + pl.program_id(0)]
    for h in range(2):
        cols = slice(h * HALF, (h + 1) * HALF)
        mine = sel[0] == h
        near, pair, cross = (jnp.where(mine, a[...], b[...]).astype(F32) for a, b in zip(own, other))
        grad = near + jnp.where(rank < 2, pair, jnp.where(rank < FAR, cross, 0.0))
        new_w[:, :, cols], new_m[:, :, cols], new_s[:, :, cols] = adam_step(
            weight[:, :, cols], moment[:, :, cols], square[:, :, cols], grad
        )


def adam(sel, weight, moment, square, own, other):
    n, r, c = weight.shape
    state = pl.BlockSpec((1, r, c), lambda i, s: (i, 0, 0))
    sums = [
        pl.BlockSpec((1, r, HALF), lambda i, s: (i, 0, 0)),
        pl.BlockSpec((1, r, HALF), lambda i, s: (jnp.clip(s[1 + i], 0, 1), 0, 0)),
        pl.BlockSpec((1, r, HALF), lambda i, s: (jnp.clip(s[1 + i] - 2, 0, 1), 0, 0)),
    ]
    return pl.pallas_call(
        adam_kernel,
        grid_spec=pltpu.PrefetchScalarGridSpec(
            num_scalar_prefetch=1,
            grid=(n,),
            in_specs=[state] * 3 + sums + sums,
            out_specs=[state] * 3,
        ),
        out_shape=[jax.ShapeDtypeStruct((n, r, c), F32)] * 3,
        compiler_params=params(),
        cost_estimate=LONG,
        name="adam",
    )(sel, weight, moment, square, *own, *other)


def rows_of(w, flip):
    return jnp.concatenate([w[y ^ flip, i] for i in range(w.shape[1]) for y in range(2)], axis=0)


def put_rows(out, v, flip):
    r = out.shape[2]
    for i in range(out.shape[1]):
        for y in range(2):
            out[y ^ flip, i] = v[(2 * i + y) * r : (2 * i + y + 1) * r].astype(BF)


def call(kernel, core, args, in_specs, out_shape, out_specs, steps, name, cost=SHORT):
    return pl.pallas_call(
        kernel,
        grid_spec=pltpu.PrefetchScalarGridSpec(
            num_scalar_prefetch=1, grid=(steps,), in_specs=in_specs, out_specs=out_specs
        ),
        out_shape=out_shape,
        compiler_params=params(56),
        cost_estimate=cost,
        name=name,
    )(core, *args)


def hidden_kernel(core, x, own, oth, hidden, hidden_t, active, steep):
    one, two = dot(x[...], rows_of(own, core[1])), dot(x[...], rows_of(oth, core[1]))
    is0 = core[0] == 0
    gating, upward = jnp.where(is0, one, two), jnp.where(is0, two, one)
    logistic = jax.nn.sigmoid(gating)
    act = gating * logistic
    hid = act * upward
    hidden[...] = hid.astype(BF)
    hidden_t[...] = hid.T.astype(BF)
    active[...] = act
    steep[...] = upward * (logistic * (1.0 + gating * (1.0 - logistic)))


def other_hidden_kernel(core, x, own, oth, hidden_t):
    one, two = dot(x[...], rows_of(own, core[1])), dot(x[...], rows_of(oth, core[1]))
    is0 = core[0] == 0
    gating, upward = jnp.where(is0, one, two), jnp.where(is0, two, one)
    hidden_t[...] = (gating * jax.nn.sigmoid(gating) * upward).T.astype(BF)


def other_hidden_of(core, got, own, oth):
    w = pl.BlockSpec((2, 16, 64, 256), lambda j, s: (0, 0, 0, j))
    return call(
        other_hidden_kernel,
        core,
        (got, own, oth),
        [pl.BlockSpec((ROWS, D), lambda j, s: (0, 0)), w, w],
        jax.ShapeDtypeStruct((FF, ROWS), BF),
        pl.BlockSpec((256, ROWS), lambda j, s: (j, 0)),
        FF // 256,
        "other_hidden",
    )


def hidden_of(core, got, own, oth):
    w = pl.BlockSpec((2, 16, 64, 256), lambda j, s: (0, 0, 0, j))
    tile = pl.BlockSpec((ROWS, 256), lambda j, s: (0, j))
    return call(
        hidden_kernel,
        core,
        (got, own, oth),
        [pl.BlockSpec((ROWS, D), lambda j, s: (0, 0)), w, w],
        [
            jax.ShapeDtypeStruct((ROWS, FF), BF),
            jax.ShapeDtypeStruct((FF, ROWS), BF),
            jax.ShapeDtypeStruct((ROWS, FF), F32),
            jax.ShapeDtypeStruct((ROWS, FF), F32),
        ],
        [tile, pl.BlockSpec((256, ROWS), lambda j, s: (j, 0)), tile, tile],
        FF // 256,
        "hidden",
    )


def outer_kernel(core, a_t, a2_t, b, b2, out):
    put_rows(out, dot(a_t[...], b[...]) + dot(a2_t[...], b2[...]), core[1])


def outer(core, a_t, a2_t, b, b2, place, name):
    m, k = a_t.shape
    left = pl.BlockSpec((m, k), lambda j, s: (0, 0))
    right = pl.BlockSpec((k, 256), lambda j, s: (0, 4 * place(s[0]) + j))
    return call(
        outer_kernel,
        core,
        (a_t, a2_t, b, b2),
        [left, left, right, right],
        jax.ShapeDtypeStruct((2, 16, m // 32, HALF), BF),
        pl.BlockSpec((2, 16, m // 32, 256), lambda j, s: (0, 0, 0, j)),
        4,
        name,
    )


def flip_kernel(core, one, two, one_t, two_t):
    one_t[...] = one[...].T
    two_t[...] = two[...].T


def flip(core, one, two):
    rows = pl.BlockSpec((ROWS, 512), lambda j, s: (0, j))
    return call(
        flip_kernel,
        core,
        (one, two),
        [rows, rows],
        [jax.ShapeDtypeStruct((D, ROWS), BF)] * 2,
        [pl.BlockSpec((512, ROWS), lambda j, s: (j, 0))] * 2,
        4,
        "flip",
        LONG,
    )


def back_kernel(core, dy_own, dy_oth, own, oth, active, steep, d_own, d_oth):
    dhidden = dot_nt(dy_own[...], rows_of(own, core[1])) + dot_nt(dy_oth[...], rows_of(oth, core[1]))
    d_gate = (dhidden * steep[...]).astype(BF)
    d_up = (dhidden * active[...]).astype(BF)
    is0 = core[0] == 0
    d_own[...] = jnp.where(is0, d_gate, d_up)
    d_oth[...] = jnp.where(is0, d_up, d_gate)


def back_of(core, got, own, oth, active, steep):
    w = pl.BlockSpec((2, 4, 32, HALF), lambda j, s: (0, j, 0, 0))
    tile = pl.BlockSpec((ROWS, 256), lambda j, s: (0, j))
    return call(
        back_kernel,
        core,
        (got, got, own, oth, active, steep),
        [
            pl.BlockSpec((ROWS, HALF), lambda j, s: (0, 2 + s[0])),
            pl.BlockSpec((ROWS, HALF), lambda j, s: (0, 3 - s[0])),
            w,
            w,
            tile,
            tile,
        ],
        [jax.ShapeDtypeStruct((ROWS, FF), BF)] * 2,
        [tile, tile],
        FF // 256,
        "back",
    )


def give_kernel(core, hidden, d_own, d_oth, own_out, oth_out, own_in, oth_in, out):
    step = pl.program_id(0)

    @pl.when(step == 0)
    def _():
        out[...] = dot(hidden[...], rows_of(own_out, core[1])).astype(BF)

    @pl.when(step == 1)
    def _():
        out[...] = dot(hidden[...], rows_of(oth_out, core[1])).astype(BF)

    @pl.when(step >= 2)
    def _():
        dx = dot_nt(d_own[...], rows_of(own_in, core[1])) + dot_nt(d_oth[...], rows_of(oth_in, core[1]))
        out[...] = dx.astype(BF)


def give_of(core, hidden, d_own, d_oth, own_out, oth_out, own_in, oth_in):
    row = pl.BlockSpec((ROWS, FF), lambda j, s: (0, 0))
    w_out = pl.BlockSpec((2, 16, 32, HALF), lambda j, s: (0, 0, 0, 0))
    w_in = pl.BlockSpec((2, 8, 64, HALF), lambda j, s: (0, jnp.maximum(j - 2, 0), 0, 0))
    return call(
        give_kernel,
        core,
        (hidden, d_own, d_oth, own_out, oth_out, own_in, oth_in),
        [row, row, row, w_out, w_out, w_in, w_in],
        jax.ShapeDtypeStruct((ROWS, 2 * D), BF),
        pl.BlockSpec(
            (ROWS, HALF), lambda j, s: (0, jnp.where(j == 0, s[0], jnp.where(j == 1, 1 - s[0], j)))
        ),
        4,
        "give",
    )


def dot(a, b):
    return jnp.dot(a, b, preferred_element_type=F32)


def dot_nt(a, b):
    return lax.dot_general(a, b, (((1,), (1,)), ((), ())), preferred_element_type=F32)


def dot_tn(a, b):
    return lax.dot_general(a, b, (((0,), (0,)), ((), ())), preferred_element_type=F32)


def over_core(v):
    return lax.ppermute(v, "core", [(0, 1), (1, 0)])


def over_pair(v):
    return lax.ppermute(v, "yl", [(0, 1), (1, 0)])


def over_cross(v):
    return lax.ppermute(v, ("yl", "yh"), [(0, 3), (3, 0), (1, 2), (2, 1)])


def on_device(
    tokens,
    cotangent,
    route_weight,
    slot_expert,
    targets,
    proj_in,
    first_in,
    second_in,
    proj_out,
    first_out,
    second_out,
):
    core = lax.axis_index("core")
    yl = lax.axis_index("yl")
    which = core[None].astype(jnp.int32)

    def after(v, *first):
        return lax.optimization_barrier((v, *first))[0]

    def spread(v):
        got = lax.all_to_all(v.reshape(32, *v.shape[-2:]), SEND_AXES, split_axis=0, concat_axis=0, tiled=True)
        return got.reshape(2, 16, *v.shape[-2:])

    def exchange(v):
        return lax.all_to_all(
            v.reshape(CHIPS, UNITS, 2 * D), CHIP_AXES, split_axis=0, concat_axis=0, tiled=True
        ).reshape(ROWS, 2 * D)

    plan, slot_rows, slot_cols = make_plan(slot_expert)

    rank, keep, spill, kept, spilt = (plan[i, :E] for i in range(5))
    ids = jnp.arange(E, dtype=jnp.int32)
    stored = (ids >> 3) == yl
    place = jnp.where(stored, (((ids >> 2) & 1) ^ core) * 4 + (ids & 3), 8 + rank)
    begin = jnp.where(stored, kept, spilt)
    length = jnp.where(stored, keep, spill)
    order = jnp.arange(HERE, dtype=jnp.int32)
    here = yl * HERE + ((order & 15) * 2 + (order >> 4))[:, None]
    index = jnp.sum(jnp.where((begin <= here) & (here < begin + length), place, 0), axis=1)
    ranked = stored & (rank == jnp.arange(FAR, dtype=jnp.int32)[:, None])
    largest = jnp.sum(jnp.where(ranked, place, 0), axis=1)
    own_rank = lax.dynamic_slice_in_dim(rank, (yl * 2 + core) * 4, 4)
    sel = jnp.concatenate([which, own_rank])

    mine, theirs = prepare(which, proj_in, proj_out)
    theirs = over_core(theirs)
    taken = take_rows(largest, mine, theirs)
    far = (over_pair(taken[0]), over_cross(taken[1]))
    send, dest = dispatch(targets, slot_rows, slot_cols, route_weight, after(tokens, *taken), cotangent)
    got = exchange(after(send, *far))
    for_in = select_rows(index, (mine, theirs, *far), 0, 64)
    for_out = select_rows(index, (mine, theirs, *far), 64, 32)
    for_in, for_out, got = lax.optimization_barrier((for_in, for_out, got))
    got2 = over_core(got)
    chip = lax.axis_index("yh") * 16 + lax.axis_index("x") * 4 + lax.axis_index("z")
    crossed = (lax.dynamic_index_in_dim(index, chip, keepdims=False) >= 10).astype(jnp.int32)
    which = jnp.stack([which[0], crossed])
    x_t, x2_t = flip(which, got, got2)
    own_in = spread(for_in)
    oth_in = over_core(own_in)
    own_out = spread(after(for_out, own_in))

    hidden, hidden_t, active, steep = hidden_of(which, got, own_in, oth_in)
    hidden2_t = other_hidden_of(which, got2, own_in, oth_in)
    grad_out = outer(which, hidden_t, hidden2_t, got, got2, lambda c: 2 + c, "outer_out")
    grad_out, own_out = lax.optimization_barrier((grad_out, own_out))
    oth_out = over_core(own_out)
    rows_out = spread(grad_out)

    d_own, d_oth = back_of(which, got, own_out, oth_out, after(active, grad_out), steep)
    d2_own = over_core(d_oth)
    grad_in = outer(which, x_t, x2_t, d_own, d2_own, lambda c: 0, "outer_in")
    rows_in = spread(after(grad_in, rows_out))

    def gather_sums(rows):
        near, near_other, pair, cross = sum_rows(index, rows.reshape(32, *rows.shape[2:]))
        pair, cross = over_pair(pair), over_cross(cross)
        own, other = (near, pair, cross), (over_core(near_other), over_core(pair), over_core(cross))
        return own, other

    result = give_of(which, hidden, d_own, d_oth, own_out, oth_out, own_in, oth_in)
    own, other = gather_sums(after(rows_out, result))
    trained_out, mean_out, square_out = adam(sel, proj_out, first_out, second_out, own, other)
    own2, other2 = gather_sums(after(rows_in, result))
    back = exchange(after(result, *own2[1:]))
    trained_in, mean_in, square_in = adam(sel, proj_in, first_in, second_in, own2, other2)
    mixed, token_grad, mix_grad = combine(dest, route_weight, cotangent, back)
    return (
        mixed,
        token_grad,
        mix_grad,
        trained_in,
        mean_in,
        square_in,
        trained_out,
        mean_out,
        square_out,
    )


def solution(mesh):
    fine = Mesh(mesh.devices.reshape(2, 2, 4, 4, 2), ALL_AXES)
    rows = P(ALL_AXES, None)
    state = P(("yl", "core"), DEV_AXES, None)
    in_specs = (rows, rows, rows, P(), rows) + (state,) * 6
    out_specs = (rows, rows, rows) + (state,) * 6
    return jax.shard_map(on_device, mesh=fine, in_specs=in_specs, out_specs=out_specs, check_vma=False)
```

```python
import jax
import jax.numpy as jnp
from jax import lax
from jax.experimental import pallas as pl
from jax.experimental.pallas import tpu as pltpu
from jax.sharding import Mesh, PartitionSpec as P

D = 2048
FF = 1024
E = 16
CAP = 3
UNITS = 8
CHIPS = 64
ROWS = CHIPS * UNITS
HALF = 1024
HERE = 32
FAR = 4

BF = jnp.bfloat16
F32 = jnp.float32

beta_first = 0.9
beta_second = 0.95
learn_rate = 0.01
decay_rate = 0.1
adam_eps = 1e-08
bias_first = 1.0 - 0.9**10
bias_second = 1.0 - 0.95**10

CHIP_AXES = ("yl", "x", "z", "yh")
DEV_AXES = ("x", "z", "yh")
SEND_AXES = ("yh", "x", "z")
ALL_AXES = ("yl", "core", "x", "z", "yh")


def params(mib=48):
    return pltpu.CompilerParams(vmem_limit_bytes=mib * 2**20)


SHORT = pl.CostEstimate(flops=1, bytes_accessed=1, transcendentals=0)
LONG = pl.CostEstimate(flops=10**10, bytes_accessed=2 * 10**7, transcendentals=0)


def adam_step(weight, moment, square, gradient):
    new_moment = beta_first * moment + (1.0 - beta_first) * gradient
    new_square = beta_second * square + (1.0 - beta_second) * gradient * gradient
    update = (
        new_moment / bias_first / (jnp.sqrt(new_square / bias_second) + adam_eps)
        + decay_rate * weight
    )
    return (weight - learn_rate * update, new_moment, new_square)


def down(mask, value=1.0):
    return jnp.sum(jnp.where(mask, value, 0.0), axis=0, keepdims=True)


def across(mask, value=1.0):
    return jnp.sum(jnp.where(mask, value, 0.0), axis=1, keepdims=True)


def grids():
    sub = lax.broadcasted_iota(jnp.int32, (128, 128), 0).astype(F32)
    lane = lax.broadcasted_iota(jnp.int32, (128, 128), 1).astype(F32)
    return sub, lane


def plan_kernel(ecol, erow, plan, slot_rows, slot_cols):
    sub, lane = grids()
    ec, er = ecol[...].astype(F32), erow[...].astype(F32)

    chips_r = jnp.floor((CAP * down(ec == lane) + (UNITS - 1)) / UNITS)
    chips_c = jnp.floor((CAP * across(er == sub) + (UNITS - 1)) / UNITS)
    expert = (sub < E) & (lane < E)
    low_s, low_l = sub < E // 2, lane < E // 2
    same = expert & (low_s == low_l)
    ahead_r = same & ((chips_c > chips_r) | ((chips_c == chips_r) & (sub < lane)))
    ahead_c = same & ((chips_r > chips_c) | ((chips_r == chips_c) & (lane < sub)))
    rank_r = down(ahead_r)
    over_r = jnp.maximum(down(same, chips_c) - HERE, 0.0)
    over_c = jnp.maximum(across(same, chips_r) - HERE, 0.0)
    spill_r = jnp.clip(over_r - down(ahead_r, chips_c), 0.0, chips_r)
    spill_c = jnp.clip(over_c - across(ahead_c, chips_r), 0.0, chips_c)
    keep_r, keep_c = chips_r - spill_r, chips_c - spill_c
    across_y = expert & (low_s != low_l)
    kept_r = down(same & (sub < lane), keep_c)
    kept_c = across(same & (lane < sub), keep_r)
    spilt_r = down(across_y, keep_c) + down(same & (sub < lane), spill_c)
    spilt_c = across(across_y, keep_r) + across(same & (lane < sub), spill_r)
    y_r = jnp.where(low_l[0:1, :], 0.0, 1.0 * HERE)
    y_c = jnp.where(low_s[:, 0:1], 0.0, 1.0 * HERE)
    kept_r, kept_c = kept_r + y_r, kept_c + y_c
    spilt_r, spilt_c = spilt_r + (HERE - y_r), spilt_c + (HERE - y_c)
    for i, v in enumerate((rank_r, keep_r, spill_r, kept_r, spilt_r)):
        plan[i : i + 1, :] = v.astype(jnp.int32)

    mine_c, mine_r = ec == lane, er == sub
    slot_cols[:, 0:1] = CAP * across((ec == er) & (lane < sub))
    slot_rows[0:1, :] = CAP * down((ec == er) & (sub < lane))
    for i, (r, c) in enumerate(((keep_r, keep_c), (kept_r, kept_c), (spilt_r - keep_r, spilt_c - keep_c))):
        slot_cols[:, i + 1 : i + 2] = UNITS * across(mine_c, r)
        slot_rows[i + 1 : i + 2, :] = UNITS * down(mine_r, c)


def make_plan(slot_expert):
    return pl.pallas_call(
        plan_kernel,
        out_shape=(
            jax.ShapeDtypeStruct((8, 128), jnp.int32),
            jax.ShapeDtypeStruct((8, 128), F32),
            jax.ShapeDtypeStruct((128, 8), F32),
        ),
        compiler_params=params(),
        name="plan",
    )(slot_expert.reshape(128, 1), slot_expert.reshape(1, 128))


def dispatch_kernel(tcol, trow, slot_rows, slot_cols, wrow, tok, cot, send, dest):
    sub, lane = grids()
    tc = [tcol[:, k : k + 1].astype(F32) for k in range(2)]
    tr = [trow[k : k + 1, :].astype(F32) for k in range(2)]
    dest_row = []
    for k in range(2):
        at = sub == tr[k]
        pos = down((tc[0] == tr[k]) & (sub < lane)) + down((tc[1] == tr[k]) & (sub < lane))
        slot, limit, first, rest = (down(at, slot_cols[:, i : i + 1]) for i in range(4))
        unit = slot + pos
        row = unit + jnp.where(unit < limit, first, rest)
        dest_row.append(jnp.where(pos < CAP, row, 4.0 * ROWS))
        at = lane == tc[k]
        pos = across((tc[k] == tr[0]) & (lane < sub)) + across((tc[k] == tr[1]) & (lane < sub))
        slot, limit, first, rest = (across(at, slot_rows[i : i + 1, :]) for i in range(4))
        unit = slot + pos
        row = unit + jnp.where(unit < limit, first, rest)
        dest[:, k : k + 1] = jnp.where(pos < CAP, row, 4.0 * ROWS)

    w0, w1 = wrow[0:1, :], wrow[1:2, :]
    for part in range(ROWS // 128):
        place = sub + 128.0 * part
        first, second = place == dest_row[0], place == dest_row[1]
        pick = jnp.where(first | second, 1.0, 0.0).astype(BF)
        weight = across(first, w0) + across(second, w1)
        rows = slice(part * 128, part * 128 + 128)
        send[rows, :D] = jnp.dot(pick, tok[...], preferred_element_type=F32).astype(BF)
        send[rows, D:] = (jnp.dot(pick, cot[...], preferred_element_type=F32) * weight).astype(BF)


def dispatch(targets, slot_rows, slot_cols, route_weight, tokens, cotangent):
    return pl.pallas_call(
        dispatch_kernel,
        out_shape=(
            jax.ShapeDtypeStruct((ROWS, 2 * D), BF),
            jax.ShapeDtypeStruct((128, 2), F32),
        ),
        compiler_params=params(),
        name="dispatch",
    )(targets, targets.T, slot_rows, slot_cols, route_weight.T, tokens, cotangent)


def combine_kernel(dest, weight, cot, out, dx, mixed, grad, mix):
    step = pl.program_id(0)
    place = lax.broadcasted_iota(jnp.int32, (128, ROWS), 1).astype(F32)
    first, second = place == dest[:, 0:1], place == dest[:, 1:2]
    pick0 = jnp.where(first, 1.0, 0.0).astype(BF)
    pick1 = jnp.where(second, 1.0, 0.0).astype(BF)
    both = jnp.where(first | second, 1.0, 0.0).astype(BF)
    out0, out1 = dot(pick0, out[...]), dot(pick1, out[...])
    here = cot[...].astype(F32)
    mixed[...] = (weight[:, 0:1] * out0 + weight[:, 1:2] * out1).astype(BF)
    grad[...] = dot(both, dx[...]).astype(BF)

    @pl.when(step == 0)
    def _():
        mix[...] = jnp.zeros_like(mix)

    mix[:, 0:1] += jnp.sum(here * out0, axis=1, keepdims=True)
    mix[:, 1:2] += jnp.sum(here * out1, axis=1, keepdims=True)


def combine(dest, route_weight, cotangent, back):
    width = 512
    whole = pl.BlockSpec((128, 2), lambda j: (0, 0))
    tile = pl.BlockSpec((128, width), lambda j: (0, j))
    return pl.pallas_call(
        combine_kernel,
        grid=(D // width,),
        in_specs=[
            whole,
            whole,
            tile,
            pl.BlockSpec((ROWS, width), lambda j: (0, j)),
            pl.BlockSpec((ROWS, width), lambda j: (0, D // width + j)),
        ],
        out_specs=[tile, tile, whole],
        out_shape=(
            jax.ShapeDtypeStruct((128, D), BF),
            jax.ShapeDtypeStruct((128, D), BF),
            jax.ShapeDtypeStruct((128, 2), F32),
        ),
        compiler_params=params(),
        name="combine",
    )(dest, route_weight, cotangent, back, back)


def prepare_kernel(core, w_in, w_out, mine, theirs):
    left_in, right_in = w_in[:, :, :HALF].astype(BF), w_in[:, :, HALF:].astype(BF)
    left_out, right_out = w_out[:, :, :HALF].astype(BF), w_out[:, :, HALF:].astype(BF)

    def put(left, right):
        left[:, :64], right[:, :64] = left_in, right_in
        left[:, 64:], right[:, 64:] = left_out, right_out

    @pl.when(core[0] == 0)
    def _():
        put(mine, theirs)

    @pl.when(core[0] != 0)
    def _():
        put(theirs, mine)


def prepare(core, w_in, w_out):
    n, r, c = w_in.shape
    ro = w_out.shape[1]
    half = pl.BlockSpec((1, r + ro, HALF), lambda i, s: (i, 0, 0))
    return pl.pallas_call(
        prepare_kernel,
        grid_spec=pltpu.PrefetchScalarGridSpec(
            num_scalar_prefetch=1,
            grid=(n,),
            in_specs=[
                pl.BlockSpec((1, r, c), lambda i, s: (i, 0, 0)),
                pl.BlockSpec((1, ro, c), lambda i, s: (i, 0, 0)),
            ],
            out_specs=[half, half],
        ),
        out_shape=[jax.ShapeDtypeStruct((n, r + ro, HALF), BF)] * 2,
        compiler_params=params(),
        name="prepare",
    )(core, pltpu.with_memory_space_constraint(w_in, pltpu.HBM), pltpu.with_memory_space_constraint(w_out, pltpu.HBM))


def copy_one(e, parts, out, j):
    start = 0
    for part in parts:
        n = part.shape[0]

        @pl.when((e >= start) & (e < start + n))
        def _(start=start, n=n, part=part):
            out[j] = part[jnp.clip(e - start, 0, n - 1)]

        start += n


def take_kernel(index, mine, theirs, pair, cross):
    for j in range(FAR):
        copy_one(index[j], (mine, theirs), (pair, cross)[j // 2], j % 2)


def take_rows(index, mine, theirs):
    n, r, c = mine.shape
    whole = pl.BlockSpec((n, r, c), lambda i, s: (0, 0, 0))
    two = pl.BlockSpec((2, r, c), lambda i, s: (0, 0, 0))
    return pl.pallas_call(
        take_kernel,
        grid_spec=pltpu.PrefetchScalarGridSpec(
            num_scalar_prefetch=1, grid=(1,), in_specs=[whole] * 2, out_specs=[two] * 2
        ),
        out_shape=[jax.ShapeDtypeStruct((2, r, c), BF)] * 2,
        compiler_params=params(),
        name="take_rows",
    )(index, mine, theirs)


def select_kernel(index, *refs):
    step = pl.program_id(0)
    for j in range(8):
        copy_one(index[step * 8 + j], refs[:-1], refs[-1], j)


def select_rows(index, parts, start, r):
    c = parts[0].shape[2]
    return pl.pallas_call(
        select_kernel,
        grid_spec=pltpu.PrefetchScalarGridSpec(
            num_scalar_prefetch=1,
            grid=(4,),
            in_specs=[pl.BlockSpec((p.shape[0], r, c), lambda i, s: (0, start // r, 0)) for p in parts],
            out_specs=pl.BlockSpec((8, r, c), lambda i, s: (i, 0, 0)),
        ),
        out_shape=jax.ShapeDtypeStruct((32, r, c), BF),
        compiler_params=params(),
        name="select_rows",
    )(index, *parts)


def sum_kernel(index, rows, mine, theirs, pair, cross, total):
    total[...] = jnp.zeros_like(total)
    for d in range(32):
        e = index[d]
        total[e] += rows[d].astype(F32)
    mine[...] = total[:4].astype(BF)
    theirs[...] = total[4:8].astype(BF)
    pair[...] = total[8:10].astype(BF)
    cross[...] = total[10:].astype(BF)


def sum_rows(index, rows):
    n, r, c = rows.shape
    step = 16
    counts = (4, 4, 2, 2)
    return pl.pallas_call(
        sum_kernel,
        grid_spec=pltpu.PrefetchScalarGridSpec(
            num_scalar_prefetch=1,
            grid=(r // step,),
            in_specs=[pl.BlockSpec((n, step, c), lambda i, s: (0, i, 0))],
            out_specs=[pl.BlockSpec((k, step, c), lambda i, s: (0, i, 0)) for k in counts],
            scratch_shapes=[pltpu.VMEM((8 + FAR, step, c), F32)],
        ),
        out_shape=[jax.ShapeDtypeStruct((k, r, c), BF) for k in counts],
        compiler_params=params(),
        cost_estimate=LONG,
        name="sum_rows",
    )(index, rows)


def adam_kernel(sel, weight, moment, square, *refs):
    own, other = refs[:3], refs[3:6]
    new_w, new_m, new_s = refs[6:]
    rank = sel[1 + pl.program_id(0)]
    for h in range(2):
        cols = slice(h * HALF, (h + 1) * HALF)
        mine = sel[0] == h
        near, pair, cross = (jnp.where(mine, a[...], b[...]).astype(F32) for a, b in zip(own, other))
        grad = near + jnp.where(rank < 2, pair, jnp.where(rank < FAR, cross, 0.0))
        new_w[:, :, cols], new_m[:, :, cols], new_s[:, :, cols] = adam_step(
            weight[:, :, cols], moment[:, :, cols], square[:, :, cols], grad
        )


def adam(sel, weight, moment, square, own, other):
    n, r, c = weight.shape
    state = pl.BlockSpec((1, r, c), lambda i, s: (i, 0, 0))
    sums = [
        pl.BlockSpec((1, r, HALF), lambda i, s: (i, 0, 0)),
        pl.BlockSpec((1, r, HALF), lambda i, s: (jnp.clip(s[1 + i], 0, 1), 0, 0)),
        pl.BlockSpec((1, r, HALF), lambda i, s: (jnp.clip(s[1 + i] - 2, 0, 1), 0, 0)),
    ]
    return pl.pallas_call(
        adam_kernel,
        grid_spec=pltpu.PrefetchScalarGridSpec(
            num_scalar_prefetch=1,
            grid=(n,),
            in_specs=[state] * 3 + sums + sums,
            out_specs=[state] * 3,
        ),
        out_shape=[jax.ShapeDtypeStruct((n, r, c), F32)] * 3,
        compiler_params=params(),
        cost_estimate=LONG,
        name="adam",
    )(sel, weight, moment, square, *own, *other)


def rows_of(w, flip):
    return jnp.concatenate([w[y ^ flip, i] for i in range(w.shape[1]) for y in range(2)], axis=0)


def put_rows(out, v, flip):
    r = out.shape[2]
    for i in range(out.shape[1]):
        for y in range(2):
            out[y ^ flip, i] = v[(2 * i + y) * r : (2 * i + y + 1) * r].astype(BF)


def call(kernel, core, args, in_specs, out_shape, out_specs, steps, name, cost=SHORT):
    return pl.pallas_call(
        kernel,
        grid_spec=pltpu.PrefetchScalarGridSpec(
            num_scalar_prefetch=1, grid=(steps,), in_specs=in_specs, out_specs=out_specs
        ),
        out_shape=out_shape,
        compiler_params=params(56),
        cost_estimate=cost,
        name=name,
    )(core, *args)


def hidden_kernel(core, x, own, oth, hidden, hidden_t, active, steep):
    one, two = dot(x[...], rows_of(own, core[1])), dot(x[...], rows_of(oth, core[1]))
    is0 = core[0] == 0
    gating, upward = jnp.where(is0, one, two), jnp.where(is0, two, one)
    logistic = jax.nn.sigmoid(gating)
    act = gating * logistic
    hid = act * upward
    hidden[...] = hid.astype(BF)
    hidden_t[...] = hid.T.astype(BF)
    active[...] = act
    steep[...] = upward * (logistic * (1.0 + gating * (1.0 - logistic)))


def other_hidden_kernel(core, x, own, oth, hidden_t):
    one, two = dot(x[...], rows_of(own, core[1])), dot(x[...], rows_of(oth, core[1]))
    is0 = core[0] == 0
    gating, upward = jnp.where(is0, one, two), jnp.where(is0, two, one)
    hidden_t[...] = (gating * jax.nn.sigmoid(gating) * upward).T.astype(BF)


def other_hidden_of(core, got, own, oth):
    w = pl.BlockSpec((2, 16, 64, 256), lambda j, s: (0, 0, 0, j))
    return call(
        other_hidden_kernel,
        core,
        (got, own, oth),
        [pl.BlockSpec((ROWS, D), lambda j, s: (0, 0)), w, w],
        jax.ShapeDtypeStruct((FF, ROWS), BF),
        pl.BlockSpec((256, ROWS), lambda j, s: (j, 0)),
        FF // 256,
        "other_hidden",
    )


def hidden_of(core, got, own, oth):
    w = pl.BlockSpec((2, 16, 64, 256), lambda j, s: (0, 0, 0, j))
    tile = pl.BlockSpec((ROWS, 256), lambda j, s: (0, j))
    return call(
        hidden_kernel,
        core,
        (got, own, oth),
        [pl.BlockSpec((ROWS, D), lambda j, s: (0, 0)), w, w],
        [
            jax.ShapeDtypeStruct((ROWS, FF), BF),
            jax.ShapeDtypeStruct((FF, ROWS), BF),
            jax.ShapeDtypeStruct((ROWS, FF), F32),
            jax.ShapeDtypeStruct((ROWS, FF), F32),
        ],
        [tile, pl.BlockSpec((256, ROWS), lambda j, s: (j, 0)), tile, tile],
        FF // 256,
        "hidden",
    )


def outer_kernel(core, a_t, a2_t, b, b2, out):
    put_rows(out, dot(a_t[...], b[...]) + dot(a2_t[...], b2[...]), core[1])


def outer(core, a_t, a2_t, b, b2, place, name):
    m, k = a_t.shape
    left = pl.BlockSpec((m, k), lambda j, s: (0, 0))
    right = pl.BlockSpec((k, 256), lambda j, s: (0, 4 * place(s[0]) + j))
    return call(
        outer_kernel,
        core,
        (a_t, a2_t, b, b2),
        [left, left, right, right],
        jax.ShapeDtypeStruct((2, 16, m // 32, HALF), BF),
        pl.BlockSpec((2, 16, m // 32, 256), lambda j, s: (0, 0, 0, j)),
        4,
        name,
    )


def flip_kernel(core, one, two, one_t, two_t):
    one_t[...] = one[...].T
    two_t[...] = two[...].T


def flip(core, one, two):
    rows = pl.BlockSpec((ROWS, 512), lambda j, s: (0, j))
    return call(
        flip_kernel,
        core,
        (one, two),
        [rows, rows],
        [jax.ShapeDtypeStruct((D, ROWS), BF)] * 2,
        [pl.BlockSpec((512, ROWS), lambda j, s: (j, 0))] * 2,
        4,
        "flip",
        LONG,
    )


def back_kernel(core, dy_own, dy_oth, own, oth, active, steep, d_own, d_oth):
    dhidden = dot_nt(dy_own[...], rows_of(own, core[1])) + dot_nt(dy_oth[...], rows_of(oth, core[1]))
    d_gate = (dhidden * steep[...]).astype(BF)
    d_up = (dhidden * active[...]).astype(BF)
    is0 = core[0] == 0
    d_own[...] = jnp.where(is0, d_gate, d_up)
    d_oth[...] = jnp.where(is0, d_up, d_gate)


def back_of(core, got, own, oth, active, steep):
    w = pl.BlockSpec((2, 4, 32, HALF), lambda j, s: (0, j, 0, 0))
    tile = pl.BlockSpec((ROWS, 256), lambda j, s: (0, j))
    return call(
        back_kernel,
        core,
        (got, got, own, oth, active, steep),
        [
            pl.BlockSpec((ROWS, HALF), lambda j, s: (0, 2 + s[0])),
            pl.BlockSpec((ROWS, HALF), lambda j, s: (0, 3 - s[0])),
            w,
            w,
            tile,
            tile,
        ],
        [jax.ShapeDtypeStruct((ROWS, FF), BF)] * 2,
        [tile, tile],
        FF // 256,
        "back",
    )


def give_kernel(core, hidden, d_own, d_oth, own_out, oth_out, own_in, oth_in, out):
    step = pl.program_id(0)

    @pl.when(step == 0)
    def _():
        out[...] = dot(hidden[...], rows_of(own_out, core[1])).astype(BF)

    @pl.when(step == 1)
    def _():
        out[...] = dot(hidden[...], rows_of(oth_out, core[1])).astype(BF)

    @pl.when(step >= 2)
    def _():
        dx = dot_nt(d_own[...], rows_of(own_in, core[1])) + dot_nt(d_oth[...], rows_of(oth_in, core[1]))
        out[...] = dx.astype(BF)


def give_of(core, hidden, d_own, d_oth, own_out, oth_out, own_in, oth_in):
    row = pl.BlockSpec((ROWS, FF), lambda j, s: (0, 0))
    w_out = pl.BlockSpec((2, 16, 32, HALF), lambda j, s: (0, 0, 0, 0))
    w_in = pl.BlockSpec((2, 8, 64, HALF), lambda j, s: (0, jnp.maximum(j - 2, 0), 0, 0))
    return call(
        give_kernel,
        core,
        (hidden, d_own, d_oth, own_out, oth_out, own_in, oth_in),
        [row, row, row, w_out, w_out, w_in, w_in],
        jax.ShapeDtypeStruct((ROWS, 2 * D), BF),
        pl.BlockSpec(
            (ROWS, HALF), lambda j, s: (0, jnp.where(j == 0, s[0], jnp.where(j == 1, 1 - s[0], j)))
        ),
        4,
        "give",
    )


def dot(a, b):
    return jnp.dot(a, b, preferred_element_type=F32)


def dot_nt(a, b):
    return lax.dot_general(a, b, (((1,), (1,)), ((), ())), preferred_element_type=F32)


def dot_tn(a, b):
    return lax.dot_general(a, b, (((0,), (0,)), ((), ())), preferred_element_type=F32)


def over_core(v):
    return lax.ppermute(v, "core", [(0, 1), (1, 0)])


def over_pair(v):
    return lax.ppermute(v, "yl", [(0, 1), (1, 0)])


def over_cross(v):
    return lax.ppermute(v, ("yl", "yh"), [(0, 3), (3, 0), (1, 2), (2, 1)])


def on_device(
    tokens,
    cotangent,
    route_weight,
    slot_expert,
    targets,
    proj_in,
    first_in,
    second_in,
    proj_out,
    first_out,
    second_out,
):
    core = lax.axis_index("core")
    yl = lax.axis_index("yl")
    which = core[None].astype(jnp.int32)

    def after(v, *first):
        return lax.optimization_barrier((v, *first))[0]

    def spread(v):
        got = lax.all_to_all(v.reshape(32, *v.shape[-2:]), SEND_AXES, split_axis=0, concat_axis=0, tiled=True)
        return got.reshape(2, 16, *v.shape[-2:])

    def exchange(v):
        return lax.all_to_all(
            v.reshape(CHIPS, UNITS, 2 * D), CHIP_AXES, split_axis=0, concat_axis=0, tiled=True
        ).reshape(ROWS, 2 * D)

    plan, slot_rows, slot_cols = make_plan(slot_expert)

    rank, keep, spill, kept, spilt = (plan[i, :E] for i in range(5))
    ids = jnp.arange(E, dtype=jnp.int32)
    stored = (ids >> 3) == yl
    place = jnp.where(stored, (((ids >> 2) & 1) ^ core) * 4 + (ids & 3), 8 + rank)
    begin = jnp.where(stored, kept, spilt)
    length = jnp.where(stored, keep, spill)
    order = jnp.arange(HERE, dtype=jnp.int32)
    here = yl * HERE + ((order & 15) * 2 + (order >> 4))[:, None]
    index = jnp.sum(jnp.where((begin <= here) & (here < begin + length), place, 0), axis=1)
    ranked = stored & (rank == jnp.arange(FAR, dtype=jnp.int32)[:, None])
    largest = jnp.sum(jnp.where(ranked, place, 0), axis=1)
    own_rank = lax.dynamic_slice_in_dim(rank, (yl * 2 + core) * 4, 4)
    sel = jnp.concatenate([which, own_rank])

    mine, theirs = prepare(which, proj_in, proj_out)
    theirs = over_core(theirs)
    taken = take_rows(largest, mine, theirs)
    far = (over_pair(taken[0]), over_cross(taken[1]))
    send, dest = dispatch(targets, slot_rows, slot_cols, route_weight, after(tokens, *taken), cotangent)
    got = exchange(after(send, *far))
    for_in = select_rows(index, (mine, theirs, *far), 0, 64)
    for_out = select_rows(index, (mine, theirs, *far), 64, 32)
    for_in, for_out, got = lax.optimization_barrier((for_in, for_out, got))
    got2 = over_core(got)
    chip = lax.axis_index("yh") * 16 + lax.axis_index("x") * 4 + lax.axis_index("z")
    crossed = (lax.dynamic_index_in_dim(index, chip, keepdims=False) >= 10).astype(jnp.int32)
    which = jnp.stack([which[0], crossed])
    x_t, x2_t = flip(which, got, got2)
    own_in = spread(for_in)
    oth_in = over_core(own_in)
    own_out = spread(after(for_out, own_in))

    hidden, hidden_t, active, steep = hidden_of(which, got, own_in, oth_in)
    hidden2_t = other_hidden_of(which, got2, own_in, oth_in)
    grad_out = outer(which, hidden_t, hidden2_t, got, got2, lambda c: 2 + c, "outer_out")
    grad_out, own_out = lax.optimization_barrier((grad_out, own_out))
    oth_out = over_core(own_out)
    rows_out = spread(grad_out)

    d_own, d_oth = back_of(which, got, own_out, oth_out, after(active, grad_out), steep)
    d2_own = over_core(d_oth)
    grad_in = outer(which, x_t, x2_t, d_own, d2_own, lambda c: 0, "outer_in")
    rows_in = spread(after(grad_in, rows_out))

    def gather_sums(rows):
        near, near_other, pair, cross = sum_rows(index, rows.reshape(32, *rows.shape[2:]))
        pair, cross = over_pair(pair), over_cross(cross)
        own, other = (near, pair, cross), (over_core(near_other), over_core(pair), over_core(cross))
        return own, other

    result = give_of(which, hidden, d_own, d_oth, own_out, oth_out, own_in, oth_in)
    own, other = gather_sums(after(rows_out, result))
    trained_out, mean_out, square_out = adam(sel, proj_out, first_out, second_out, own, other)
    own2, other2 = gather_sums(after(rows_in, result, *own))
    back = exchange(after(result, *own[1:], *own2[1:]))
    trained_in, mean_in, square_in = adam(sel, proj_in, first_in, second_in, own2, other2)
    mixed, token_grad, mix_grad = combine(dest, route_weight, cotangent, back)
    return (
        mixed,
        token_grad,
        mix_grad,
        trained_in,
        mean_in,
        square_in,
        trained_out,
        mean_out,
        square_out,
    )


def solution(mesh):
    fine = Mesh(mesh.devices.reshape(2, 2, 4, 4, 2), ALL_AXES)
    rows = P(ALL_AXES, None)
    state = P(("yl", "core"), DEV_AXES, None)
    in_specs = (rows, rows, rows, P(), rows) + (state,) * 6
    out_specs = (rows, rows, rows) + (state,) * 6
    return jax.shard_map(on_device, mesh=fine, in_specs=in_specs, out_specs=out_specs, check_vma=False)
```

```python
import jax
import jax.numpy as jnp
from jax import lax
from jax.experimental import pallas as pl
from jax.experimental.pallas import tpu as pltpu
from jax.sharding import Mesh, PartitionSpec as P

D = 2048
FF = 1024
E = 16
CAP = 3
UNITS = 8
CHIPS = 64
ROWS = CHIPS * UNITS
HALF = 1024
HERE = 32
FAR = 4

BF = jnp.bfloat16
F32 = jnp.float32

beta_first = 0.9
beta_second = 0.95
learn_rate = 0.01
decay_rate = 0.1
adam_eps = 1e-08
bias_first = 1.0 - 0.9**10
bias_second = 1.0 - 0.95**10

CHIP_AXES = ("yl", "x", "z", "yh")
DEV_AXES = ("x", "z", "yh")
SEND_AXES = ("yh", "x", "z")
ALL_AXES = ("yl", "core", "x", "z", "yh")


def params(mib=48):
    return pltpu.CompilerParams(vmem_limit_bytes=mib * 2**20)


SHORT = pl.CostEstimate(flops=1, bytes_accessed=1, transcendentals=0)
LONG = pl.CostEstimate(flops=10**10, bytes_accessed=2 * 10**7, transcendentals=0)


def adam_step(weight, moment, square, gradient):
    new_moment = beta_first * moment + (1.0 - beta_first) * gradient
    new_square = beta_second * square + (1.0 - beta_second) * gradient * gradient
    update = (
        new_moment / bias_first / (jnp.sqrt(new_square / bias_second) + adam_eps)
        + decay_rate * weight
    )
    return (weight - learn_rate * update, new_moment, new_square)


def down(mask, value=1.0):
    return jnp.sum(jnp.where(mask, value, 0.0), axis=0, keepdims=True)


def across(mask, value=1.0):
    return jnp.sum(jnp.where(mask, value, 0.0), axis=1, keepdims=True)


def grids():
    sub = lax.broadcasted_iota(jnp.int32, (128, 128), 0).astype(F32)
    lane = lax.broadcasted_iota(jnp.int32, (128, 128), 1).astype(F32)
    return sub, lane


def plan_kernel(ecol, erow, plan, slot_rows, slot_cols):
    sub, lane = grids()
    ec, er = ecol[...].astype(F32), erow[...].astype(F32)

    chips_r = jnp.floor((CAP * down(ec == lane) + (UNITS - 1)) / UNITS)
    chips_c = jnp.floor((CAP * across(er == sub) + (UNITS - 1)) / UNITS)
    expert = (sub < E) & (lane < E)
    low_s, low_l = sub < E // 2, lane < E // 2
    same = expert & (low_s == low_l)
    ahead_r = same & ((chips_c > chips_r) | ((chips_c == chips_r) & (sub < lane)))
    ahead_c = same & ((chips_r > chips_c) | ((chips_r == chips_c) & (lane < sub)))
    rank_r = down(ahead_r)
    over_r = jnp.maximum(down(same, chips_c) - HERE, 0.0)
    over_c = jnp.maximum(across(same, chips_r) - HERE, 0.0)
    spill_r = jnp.clip(over_r - down(ahead_r, chips_c), 0.0, chips_r)
    spill_c = jnp.clip(over_c - across(ahead_c, chips_r), 0.0, chips_c)
    keep_r, keep_c = chips_r - spill_r, chips_c - spill_c
    across_y = expert & (low_s != low_l)
    kept_r = down(same & (sub < lane), keep_c)
    kept_c = across(same & (lane < sub), keep_r)
    spilt_r = down(across_y, keep_c) + down(same & (sub < lane), spill_c)
    spilt_c = across(across_y, keep_r) + across(same & (lane < sub), spill_r)
    y_r = jnp.where(low_l[0:1, :], 0.0, 1.0 * HERE)
    y_c = jnp.where(low_s[:, 0:1], 0.0, 1.0 * HERE)
    kept_r, kept_c = kept_r + y_r, kept_c + y_c
    spilt_r, spilt_c = spilt_r + (HERE - y_r), spilt_c + (HERE - y_c)
    for i, v in enumerate((rank_r, keep_r, spill_r, kept_r, spilt_r)):
        plan[i : i + 1, :] = v.astype(jnp.int32)

    mine_c, mine_r = ec == lane, er == sub
    slot_cols[:, 0:1] = CAP * across((ec == er) & (lane < sub))
    slot_rows[0:1, :] = CAP * down((ec == er) & (sub < lane))
    for i, (r, c) in enumerate(((keep_r, keep_c), (kept_r, kept_c), (spilt_r - keep_r, spilt_c - keep_c))):
        slot_cols[:, i + 1 : i + 2] = UNITS * across(mine_c, r)
        slot_rows[i + 1 : i + 2, :] = UNITS * down(mine_r, c)


def make_plan(slot_expert):
    return pl.pallas_call(
        plan_kernel,
        out_shape=(
            jax.ShapeDtypeStruct((8, 128), jnp.int32),
            jax.ShapeDtypeStruct((8, 128), F32),
            jax.ShapeDtypeStruct((128, 8), F32),
        ),
        compiler_params=params(),
        name="plan",
    )(slot_expert.reshape(128, 1), slot_expert.reshape(1, 128))


def dispatch_kernel(tcol, trow, slot_rows, slot_cols, wrow, tok, cot, send, dest):
    sub, lane = grids()
    tc = [tcol[:, k : k + 1].astype(F32) for k in range(2)]
    tr = [trow[k : k + 1, :].astype(F32) for k in range(2)]
    dest_row = []
    for k in range(2):
        at = sub == tr[k]
        pos = down((tc[0] == tr[k]) & (sub < lane)) + down((tc[1] == tr[k]) & (sub < lane))
        slot, limit, first, rest = (down(at, slot_cols[:, i : i + 1]) for i in range(4))
        unit = slot + pos
        row = unit + jnp.where(unit < limit, first, rest)
        dest_row.append(jnp.where(pos < CAP, row, 4.0 * ROWS))
        at = lane == tc[k]
        pos = across((tc[k] == tr[0]) & (lane < sub)) + across((tc[k] == tr[1]) & (lane < sub))
        slot, limit, first, rest = (across(at, slot_rows[i : i + 1, :]) for i in range(4))
        unit = slot + pos
        row = unit + jnp.where(unit < limit, first, rest)
        dest[:, k : k + 1] = jnp.where(pos < CAP, row, 4.0 * ROWS)

    w0, w1 = wrow[0:1, :], wrow[1:2, :]
    for part in range(ROWS // 128):
        place = sub + 128.0 * part
        first, second = place == dest_row[0], place == dest_row[1]
        pick = jnp.where(first | second, 1.0, 0.0).astype(BF)
        weight = across(first, w0) + across(second, w1)
        rows = slice(part * 128, part * 128 + 128)
        send[rows, :D] = jnp.dot(pick, tok[...], preferred_element_type=F32).astype(BF)
        send[rows, D:] = (jnp.dot(pick, cot[...], preferred_element_type=F32) * weight).astype(BF)


def dispatch(targets, slot_rows, slot_cols, route_weight, tokens, cotangent):
    return pl.pallas_call(
        dispatch_kernel,
        out_shape=(
            jax.ShapeDtypeStruct((ROWS, 2 * D), BF),
            jax.ShapeDtypeStruct((128, 2), F32),
        ),
        compiler_params=params(),
        name="dispatch",
    )(targets, targets.T, slot_rows, slot_cols, route_weight.T, tokens, cotangent)


def picks(dest):
    place = lax.broadcasted_iota(jnp.int32, (128, ROWS), 1).astype(F32)
    return place == dest[:, 0:1], place == dest[:, 1:2]


def mix_kernel(dest, weight, cot, out, mixed, mix):
    first, second = picks(dest)
    pick0 = jnp.where(first, 1.0, 0.0).astype(BF)
    pick1 = jnp.where(second, 1.0, 0.0).astype(BF)
    w0, w1 = weight[:, 0:1], weight[:, 1:2]
    mix0 = jnp.zeros((128, 1), F32)
    mix1 = jnp.zeros((128, 1), F32)
    for c in range(0, D, 512):
        cols = slice(c, c + 512)
        out0, out1 = dot(pick0, out[:, cols]), dot(pick1, out[:, cols])
        here = cot[:, cols].astype(F32)
        mixed[:, cols] = (w0 * out0 + w1 * out1).astype(BF)
        mix0 += jnp.sum(here * out0, axis=1, keepdims=True)
        mix1 += jnp.sum(here * out1, axis=1, keepdims=True)
    mix[:, 0:1] = mix0
    mix[:, 1:2] = mix1


def mix_results(dest, route_weight, cotangent, back):
    return pl.pallas_call(
        mix_kernel,
        out_shape=(
            jax.ShapeDtypeStruct((128, D), BF),
            jax.ShapeDtypeStruct((128, 2), F32),
        ),
        compiler_params=params(),
        cost_estimate=LONG,
        name="mix_results",
    )(dest, route_weight, cotangent, back)


def add_kernel(dest, dx, grad):
    first, second = picks(dest)
    both = jnp.where(first | second, 1.0, 0.0).astype(BF)
    for c in range(0, D, 512):
        grad[:, c : c + 512] = dot(both, dx[:, c : c + 512]).astype(BF)


def add_gradients(dest, back):
    return pl.pallas_call(
        add_kernel,
        out_shape=jax.ShapeDtypeStruct((128, D), BF),
        compiler_params=params(),
        name="add_gradients",
    )(dest, back)


def prepare_kernel(core, w_in, w_out, mine, theirs):
    left_in, right_in = w_in[:, :, :HALF].astype(BF), w_in[:, :, HALF:].astype(BF)
    left_out, right_out = w_out[:, :, :HALF].astype(BF), w_out[:, :, HALF:].astype(BF)

    def put(left, right):
        left[:, :64], right[:, :64] = left_in, right_in
        left[:, 64:], right[:, 64:] = left_out, right_out

    @pl.when(core[0] == 0)
    def _():
        put(mine, theirs)

    @pl.when(core[0] != 0)
    def _():
        put(theirs, mine)


def prepare(core, w_in, w_out):
    n, r, c = w_in.shape
    ro = w_out.shape[1]
    half = pl.BlockSpec((1, r + ro, HALF), lambda i, s: (i, 0, 0))
    return pl.pallas_call(
        prepare_kernel,
        grid_spec=pltpu.PrefetchScalarGridSpec(
            num_scalar_prefetch=1,
            grid=(n,),
            in_specs=[
                pl.BlockSpec((1, r, c), lambda i, s: (i, 0, 0)),
                pl.BlockSpec((1, ro, c), lambda i, s: (i, 0, 0)),
            ],
            out_specs=[half, half],
        ),
        out_shape=[jax.ShapeDtypeStruct((n, r + ro, HALF), BF)] * 2,
        compiler_params=params(),
        name="prepare",
    )(core, pltpu.with_memory_space_constraint(w_in, pltpu.HBM), pltpu.with_memory_space_constraint(w_out, pltpu.HBM))


def copy_one(e, parts, out, j):
    start = 0
    for part in parts:
        n = part.shape[0]

        @pl.when((e >= start) & (e < start + n))
        def _(start=start, n=n, part=part):
            out[j] = part[jnp.clip(e - start, 0, n - 1)]

        start += n


def take_kernel(index, mine, theirs, pair, cross):
    for j in range(FAR):
        copy_one(index[j], (mine, theirs), (pair, cross)[j // 2], j % 2)


def take_rows(index, mine, theirs):
    n, r, c = mine.shape
    whole = pl.BlockSpec((n, r, c), lambda i, s: (0, 0, 0))
    two = pl.BlockSpec((2, r, c), lambda i, s: (0, 0, 0))
    return pl.pallas_call(
        take_kernel,
        grid_spec=pltpu.PrefetchScalarGridSpec(
            num_scalar_prefetch=1, grid=(1,), in_specs=[whole] * 2, out_specs=[two] * 2
        ),
        out_shape=[jax.ShapeDtypeStruct((2, r, c), BF)] * 2,
        compiler_params=params(),
        name="take_rows",
    )(index, mine, theirs)


def select_kernel(index, *refs):
    step = pl.program_id(0)
    for j in range(8):
        copy_one(index[step * 8 + j], refs[:-1], refs[-1], j)


def select_rows(index, parts, start, r):
    c = parts[0].shape[2]
    return pl.pallas_call(
        select_kernel,
        grid_spec=pltpu.PrefetchScalarGridSpec(
            num_scalar_prefetch=1,
            grid=(4,),
            in_specs=[pl.BlockSpec((p.shape[0], r, c), lambda i, s: (0, start // r, 0)) for p in parts],
            out_specs=pl.BlockSpec((8, r, c), lambda i, s: (i, 0, 0)),
        ),
        out_shape=jax.ShapeDtypeStruct((32, r, c), BF),
        compiler_params=params(),
        name="select_rows",
    )(index, *parts)


def sum_kernel(index, rows, mine, theirs, pair, cross, total):
    total[...] = jnp.zeros_like(total)
    for d in range(32):
        e = index[d]
        total[e] += rows[d].astype(F32)
    mine[...] = total[:4].astype(BF)
    theirs[...] = total[4:8].astype(BF)
    pair[...] = total[8:10].astype(BF)
    cross[...] = total[10:].astype(BF)


def sum_rows(index, rows):
    n, r, c = rows.shape
    step = 16
    counts = (4, 4, 2, 2)
    return pl.pallas_call(
        sum_kernel,
        grid_spec=pltpu.PrefetchScalarGridSpec(
            num_scalar_prefetch=1,
            grid=(r // step,),
            in_specs=[pl.BlockSpec((n, step, c), lambda i, s: (0, i, 0))],
            out_specs=[pl.BlockSpec((k, step, c), lambda i, s: (0, i, 0)) for k in counts],
            scratch_shapes=[pltpu.VMEM((8 + FAR, step, c), F32)],
        ),
        out_shape=[jax.ShapeDtypeStruct((k, r, c), BF) for k in counts],
        compiler_params=params(),
        cost_estimate=LONG,
        name="sum_rows",
    )(index, rows)


def adam_kernel(sel, weight, moment, square, *refs):
    own, other = refs[:3], refs[3:6]
    new_w, new_m, new_s = refs[6:]
    rank = sel[1 + pl.program_id(0)]
    for h in range(2):
        cols = slice(h * HALF, (h + 1) * HALF)
        mine = sel[0] == h
        near, pair, cross = (jnp.where(mine, a[...], b[...]).astype(F32) for a, b in zip(own, other))
        grad = near + jnp.where(rank < 2, pair, jnp.where(rank < FAR, cross, 0.0))
        new_w[:, :, cols], new_m[:, :, cols], new_s[:, :, cols] = adam_step(
            weight[:, :, cols], moment[:, :, cols], square[:, :, cols], grad
        )


def adam(sel, weight, moment, square, own, other):
    n, r, c = weight.shape
    state = pl.BlockSpec((1, r, c), lambda i, s: (i, 0, 0))
    sums = [
        pl.BlockSpec((1, r, HALF), lambda i, s: (i, 0, 0)),
        pl.BlockSpec((1, r, HALF), lambda i, s: (jnp.clip(s[1 + i], 0, 1), 0, 0)),
        pl.BlockSpec((1, r, HALF), lambda i, s: (jnp.clip(s[1 + i] - 2, 0, 1), 0, 0)),
    ]
    return pl.pallas_call(
        adam_kernel,
        grid_spec=pltpu.PrefetchScalarGridSpec(
            num_scalar_prefetch=1,
            grid=(n,),
            in_specs=[state] * 3 + sums + sums,
            out_specs=[state] * 3,
        ),
        out_shape=[jax.ShapeDtypeStruct((n, r, c), F32)] * 3,
        compiler_params=params(),
        cost_estimate=LONG,
        name="adam",
    )(sel, weight, moment, square, *own, *other)


def rows_of(w, flip):
    return jnp.concatenate([w[y ^ flip, i] for i in range(w.shape[1]) for y in range(2)], axis=0)


def put_rows(out, v, flip):
    r = out.shape[2]
    for i in range(out.shape[1]):
        for y in range(2):
            out[y ^ flip, i] = v[(2 * i + y) * r : (2 * i + y + 1) * r].astype(BF)


def call(kernel, core, args, in_specs, out_shape, out_specs, steps, name, cost=SHORT):
    return pl.pallas_call(
        kernel,
        grid_spec=pltpu.PrefetchScalarGridSpec(
            num_scalar_prefetch=1, grid=(steps,), in_specs=in_specs, out_specs=out_specs
        ),
        out_shape=out_shape,
        compiler_params=params(56),
        cost_estimate=cost,
        name=name,
    )(core, *args)


def hidden_kernel(core, x, own, oth, hidden, hidden_t, active, steep):
    one, two = dot(x[...], rows_of(own, core[1])), dot(x[...], rows_of(oth, core[1]))
    is0 = core[0] == 0
    gating, upward = jnp.where(is0, one, two), jnp.where(is0, two, one)
    logistic = jax.nn.sigmoid(gating)
    act = gating * logistic
    hid = act * upward
    hidden[...] = hid.astype(BF)
    hidden_t[...] = hid.T.astype(BF)
    active[...] = act
    steep[...] = upward * (logistic * (1.0 + gating * (1.0 - logistic)))


def other_hidden_kernel(core, x, own, oth, hidden_t):
    one, two = dot(x[...], rows_of(own, core[1])), dot(x[...], rows_of(oth, core[1]))
    is0 = core[0] == 0
    gating, upward = jnp.where(is0, one, two), jnp.where(is0, two, one)
    hidden_t[...] = (gating * jax.nn.sigmoid(gating) * upward).T.astype(BF)


def other_hidden_of(core, got, own, oth):
    w = pl.BlockSpec((2, 16, 64, 256), lambda j, s: (0, 0, 0, j))
    return call(
        other_hidden_kernel,
        core,
        (got, own, oth),
        [pl.BlockSpec((ROWS, D), lambda j, s: (0, 0)), w, w],
        jax.ShapeDtypeStruct((FF, ROWS), BF),
        pl.BlockSpec((256, ROWS), lambda j, s: (j, 0)),
        FF // 256,
        "other_hidden",
    )


def hidden_of(core, got, own, oth):
    w = pl.BlockSpec((2, 16, 64, 256), lambda j, s: (0, 0, 0, j))
    tile = pl.BlockSpec((ROWS, 256), lambda j, s: (0, j))
    return call(
        hidden_kernel,
        core,
        (got, own, oth),
        [pl.BlockSpec((ROWS, D), lambda j, s: (0, 0)), w, w],
        [
            jax.ShapeDtypeStruct((ROWS, FF), BF),
            jax.ShapeDtypeStruct((FF, ROWS), BF),
            jax.ShapeDtypeStruct((ROWS, FF), F32),
            jax.ShapeDtypeStruct((ROWS, FF), F32),
        ],
        [tile, pl.BlockSpec((256, ROWS), lambda j, s: (j, 0)), tile, tile],
        FF // 256,
        "hidden",
    )


def outer_kernel(core, a_t, a2_t, b, b2, out):
    put_rows(out, dot(a_t[...], b[...]) + dot(a2_t[...], b2[...]), core[1])


def outer(core, a_t, a2_t, b, b2, place, name):
    m, k = a_t.shape
    left = pl.BlockSpec((m, k), lambda j, s: (0, 0))
    right = pl.BlockSpec((k, 256), lambda j, s: (0, 4 * place(s[0]) + j))
    return call(
        outer_kernel,
        core,
        (a_t, a2_t, b, b2),
        [left, left, right, right],
        jax.ShapeDtypeStruct((2, 16, m // 32, HALF), BF),
        pl.BlockSpec((2, 16, m // 32, 256), lambda j, s: (0, 0, 0, j)),
        4,
        name,
    )


def flip_kernel(core, one, two, one_t, two_t):
    one_t[...] = one[...].T
    two_t[...] = two[...].T


def flip(core, one, two):
    rows = pl.BlockSpec((ROWS, 512), lambda j, s: (0, j))
    return call(
        flip_kernel,
        core,
        (one, two),
        [rows, rows],
        [jax.ShapeDtypeStruct((D, ROWS), BF)] * 2,
        [pl.BlockSpec((512, ROWS), lambda j, s: (j, 0))] * 2,
        4,
        "flip",
        LONG,
    )


def back_kernel(core, dy_own, dy_oth, own, oth, active, steep, d_own, d_oth):
    dhidden = dot_nt(dy_own[...], rows_of(own, core[1])) + dot_nt(dy_oth[...], rows_of(oth, core[1]))
    d_gate = (dhidden * steep[...]).astype(BF)
    d_up = (dhidden * active[...]).astype(BF)
    is0 = core[0] == 0
    d_own[...] = jnp.where(is0, d_gate, d_up)
    d_oth[...] = jnp.where(is0, d_up, d_gate)


def back_of(core, got, own, oth, active, steep):
    w = pl.BlockSpec((2, 4, 32, HALF), lambda j, s: (0, j, 0, 0))
    tile = pl.BlockSpec((ROWS, 256), lambda j, s: (0, j))
    return call(
        back_kernel,
        core,
        (got, got, own, oth, active, steep),
        [
            pl.BlockSpec((ROWS, HALF), lambda j, s: (0, 2 + s[0])),
            pl.BlockSpec((ROWS, HALF), lambda j, s: (0, 3 - s[0])),
            w,
            w,
            tile,
            tile,
        ],
        [jax.ShapeDtypeStruct((ROWS, FF), BF)] * 2,
        [tile, tile],
        FF // 256,
        "back",
    )


def result_kernel(core, hidden, own, oth, out):
    step = pl.program_id(0)

    @pl.when(step == 0)
    def _():
        out[...] = dot(hidden[...], rows_of(own, core[1])).astype(BF)

    @pl.when(step == 1)
    def _():
        out[...] = dot(hidden[...], rows_of(oth, core[1])).astype(BF)


def result_of(core, hidden, own, oth):
    w = pl.BlockSpec((2, 16, 32, HALF), lambda j, s: (0, 0, 0, 0))
    return call(
        result_kernel,
        core,
        (hidden, own, oth),
        [pl.BlockSpec((ROWS, FF), lambda j, s: (0, 0)), w, w],
        jax.ShapeDtypeStruct((ROWS, D), BF),
        pl.BlockSpec((ROWS, HALF), lambda j, s: (0, jnp.where(j == 0, s[0], 1 - s[0]))),
        2,
        "result",
        LONG,
    )


def dx_kernel(core, d_own, d_oth, own, oth, out):
    dx = dot_nt(d_own[...], rows_of(own, core[1])) + dot_nt(d_oth[...], rows_of(oth, core[1]))
    out[...] = dx.astype(BF)


def dx_of(core, d_own, d_oth, own, oth):
    row = pl.BlockSpec((ROWS, FF), lambda j, s: (0, 0))
    w = pl.BlockSpec((2, 4, 64, HALF), lambda j, s: (0, j, 0, 0))
    return call(
        dx_kernel,
        core,
        (d_own, d_oth, own, oth),
        [row, row, w, w],
        jax.ShapeDtypeStruct((ROWS, D), BF),
        pl.BlockSpec((ROWS, 512), lambda j, s: (0, j)),
        4,
        "dx",
        LONG,
    )


def dot(a, b):
    return jnp.dot(a, b, preferred_element_type=F32)


def dot_nt(a, b):
    return lax.dot_general(a, b, (((1,), (1,)), ((), ())), preferred_element_type=F32)


def over_core(v):
    return lax.ppermute(v, "core", [(0, 1), (1, 0)])


def over_pair(v):
    return lax.ppermute(v, "yl", [(0, 1), (1, 0)])


def over_cross(v):
    return lax.ppermute(v, ("yl", "yh"), [(0, 3), (3, 0), (1, 2), (2, 1)])


def on_device(
    tokens,
    cotangent,
    route_weight,
    slot_expert,
    targets,
    proj_in,
    first_in,
    second_in,
    proj_out,
    first_out,
    second_out,
):
    core = lax.axis_index("core")
    yl = lax.axis_index("yl")
    which = core[None].astype(jnp.int32)

    def after(v, *first):
        return lax.optimization_barrier((v, *first))[0]

    def spread(v):
        got = lax.all_to_all(v.reshape(32, *v.shape[-2:]), SEND_AXES, split_axis=0, concat_axis=0, tiled=True)
        return got.reshape(2, 16, *v.shape[-2:])

    def exchange(v):
        return lax.all_to_all(
            v.reshape(CHIPS, UNITS, -1), CHIP_AXES, split_axis=0, concat_axis=0, tiled=True
        ).reshape(v.shape)

    plan, slot_rows, slot_cols = make_plan(slot_expert)

    rank, keep, spill, kept, spilt = (plan[i, :E] for i in range(5))
    ids = jnp.arange(E, dtype=jnp.int32)
    stored = (ids >> 3) == yl
    place = jnp.where(stored, (((ids >> 2) & 1) ^ core) * 4 + (ids & 3), 8 + rank)
    begin = jnp.where(stored, kept, spilt)
    length = jnp.where(stored, keep, spill)
    order = jnp.arange(HERE, dtype=jnp.int32)
    here = yl * HERE + ((order & 15) * 2 + (order >> 4))[:, None]
    index = jnp.sum(jnp.where((begin <= here) & (here < begin + length), place, 0), axis=1)
    ranked = stored & (rank == jnp.arange(FAR, dtype=jnp.int32)[:, None])
    largest = jnp.sum(jnp.where(ranked, place, 0), axis=1)
    own_rank = lax.dynamic_slice_in_dim(rank, (yl * 2 + core) * 4, 4)
    sel = jnp.concatenate([which, own_rank])

    mine, theirs = prepare(which, proj_in, proj_out)
    theirs = over_core(theirs)
    taken = take_rows(largest, mine, theirs)
    far = (over_pair(taken[0]), over_cross(taken[1]))
    send, dest = dispatch(targets, slot_rows, slot_cols, route_weight, after(tokens, *taken), cotangent)
    got = exchange(after(send, *far))
    for_in = select_rows(index, (mine, theirs, *far), 0, 64)
    for_out = select_rows(index, (mine, theirs, *far), 64, 32)
    for_in, for_out, got = lax.optimization_barrier((for_in, for_out, got))
    got2 = over_core(got)
    chip = lax.axis_index("yh") * 16 + lax.axis_index("x") * 4 + lax.axis_index("z")
    crossed = (lax.dynamic_index_in_dim(index, chip, keepdims=False) >= 10).astype(jnp.int32)
    which = jnp.stack([which[0], crossed])
    x_t, x2_t = flip(which, got, got2)
    own_in = spread(for_in)
    oth_in = over_core(own_in)
    own_out = spread(after(for_out, own_in))

    hidden, hidden_t, active, steep = hidden_of(which, got, own_in, oth_in)
    hidden2_t = other_hidden_of(which, got2, own_in, oth_in)
    grad_out = outer(which, hidden_t, hidden2_t, got, got2, lambda c: 2 + c, "outer_out")
    grad_out, own_out = lax.optimization_barrier((grad_out, own_out))
    oth_out = over_core(own_out)
    rows_out = spread(grad_out)

    d_own, d_oth = back_of(which, got, own_out, oth_out, after(active, grad_out), steep)
    d2_own = over_core(d_oth)
    grad_in = outer(which, x_t, x2_t, d_own, d2_own, lambda c: 0, "outer_in")
    rows_in = spread(after(grad_in, rows_out))

    def gather_sums(rows):
        near, near_other, pair, cross = sum_rows(index, rows.reshape(32, *rows.shape[2:]))
        pair, cross = over_pair(pair), over_cross(cross)
        own, other = (near, pair, cross), (over_core(near_other), over_core(pair), over_core(cross))
        return own, other

    result = result_of(which, hidden, own_out, oth_out)
    rows_dx = dx_of(which, d_own, d_oth, own_in, oth_in)
    own, other = gather_sums(after(rows_out, result, rows_dx))
    trained_out, mean_out, square_out = adam(sel, proj_out, first_out, second_out, own, other)
    rows_in = after(rows_in, result, rows_dx, *own)
    back = exchange(after(result, rows_in))
    own2, other2 = gather_sums(rows_in)
    mixed, mix_grad = mix_results(dest, route_weight, cotangent, back)
    back_dx = exchange(after(rows_dx, back))
    own2 = (after(own2[0], back), *own2[1:])
    trained_in, mean_in, square_in = adam(sel, proj_in, first_in, second_in, own2, other2)
    token_grad = add_gradients(dest, back_dx)
    return (
        mixed,
        token_grad,
        mix_grad,
        trained_in,
        mean_in,
        square_in,
        trained_out,
        mean_out,
        square_out,
    )


def solution(mesh):
    fine = Mesh(mesh.devices.reshape(2, 2, 4, 4, 2), ALL_AXES)
    rows = P(ALL_AXES, None)
    state = P(("yl", "core"), DEV_AXES, None)
    in_specs = (rows, rows, rows, P(), rows) + (state,) * 6
    out_specs = (rows, rows, rows) + (state,) * 6
    return jax.shard_map(on_device, mesh=fine, in_specs=in_specs, out_specs=out_specs, check_vma=False)
```

```python
import jax
import jax.numpy as jnp
from jax import lax
from jax.experimental import pallas as pl
from jax.experimental.pallas import tpu as pltpu
from jax.sharding import Mesh, PartitionSpec as P

D = 2048
FF = 1024
E = 16
CAP = 3
UNITS = 8
CHIPS = 64
ROWS = CHIPS * UNITS
HALF = 1024
HERE = 32
FAR = 4

BF = jnp.bfloat16
F32 = jnp.float32

beta_first = 0.9
beta_second = 0.95
learn_rate = 0.01
decay_rate = 0.1
adam_eps = 1e-08
bias_first = 1.0 - 0.9**10
bias_second = 1.0 - 0.95**10

CHIP_AXES = ("yl", "x", "z", "yh")
DEV_AXES = ("x", "z", "yh")
SEND_AXES = ("yh", "x", "z")
ALL_AXES = ("yl", "core", "x", "z", "yh")


def params(mib=48):
    return pltpu.CompilerParams(vmem_limit_bytes=mib * 2**20)


SHORT = pl.CostEstimate(flops=1, bytes_accessed=1, transcendentals=0)
LONG = pl.CostEstimate(flops=10**10, bytes_accessed=2 * 10**7, transcendentals=0)


def adam_step(weight, moment, square, gradient):
    new_moment = beta_first * moment + (1.0 - beta_first) * gradient
    new_square = beta_second * square + (1.0 - beta_second) * gradient * gradient
    update = (
        new_moment / bias_first / (jnp.sqrt(new_square / bias_second) + adam_eps)
        + decay_rate * weight
    )
    return (weight - learn_rate * update, new_moment, new_square)


def down(mask, value=1.0):
    return jnp.sum(jnp.where(mask, value, 0.0), axis=0, keepdims=True)


def across(mask, value=1.0):
    return jnp.sum(jnp.where(mask, value, 0.0), axis=1, keepdims=True)


def grids():
    sub = lax.broadcasted_iota(jnp.int32, (128, 128), 0).astype(F32)
    lane = lax.broadcasted_iota(jnp.int32, (128, 128), 1).astype(F32)
    return sub, lane


def plan_kernel(ecol, erow, plan, slot_rows, slot_cols):
    sub, lane = grids()
    ec, er = ecol[...].astype(F32), erow[...].astype(F32)

    chips_r = jnp.floor((CAP * down(ec == lane) + (UNITS - 1)) / UNITS)
    chips_c = jnp.floor((CAP * across(er == sub) + (UNITS - 1)) / UNITS)
    expert = (sub < E) & (lane < E)
    low_s, low_l = sub < E // 2, lane < E // 2
    same = expert & (low_s == low_l)
    ahead_r = same & ((chips_c > chips_r) | ((chips_c == chips_r) & (sub < lane)))
    ahead_c = same & ((chips_r > chips_c) | ((chips_r == chips_c) & (lane < sub)))
    rank_r = down(ahead_r)
    over_r = jnp.maximum(down(same, chips_c) - HERE, 0.0)
    over_c = jnp.maximum(across(same, chips_r) - HERE, 0.0)
    spill_r = jnp.clip(over_r - down(ahead_r, chips_c), 0.0, chips_r)
    spill_c = jnp.clip(over_c - across(ahead_c, chips_r), 0.0, chips_c)
    keep_r, keep_c = chips_r - spill_r, chips_c - spill_c
    across_y = expert & (low_s != low_l)
    kept_r = down(same & (sub < lane), keep_c)
    kept_c = across(same & (lane < sub), keep_r)
    spilt_r = down(across_y, keep_c) + down(same & (sub < lane), spill_c)
    spilt_c = across(across_y, keep_r) + across(same & (lane < sub), spill_r)
    y_r = jnp.where(low_l[0:1, :], 0.0, 1.0 * HERE)
    y_c = jnp.where(low_s[:, 0:1], 0.0, 1.0 * HERE)
    kept_r, kept_c = kept_r + y_r, kept_c + y_c
    spilt_r, spilt_c = spilt_r + (HERE - y_r), spilt_c + (HERE - y_c)
    for i, v in enumerate((rank_r, keep_r, spill_r, kept_r, spilt_r)):
        plan[i : i + 1, :] = v.astype(jnp.int32)

    mine_c, mine_r = ec == lane, er == sub
    slot_cols[:, 0:1] = CAP * across((ec == er) & (lane < sub))
    slot_rows[0:1, :] = CAP * down((ec == er) & (sub < lane))
    for i, (r, c) in enumerate(((keep_r, keep_c), (kept_r, kept_c), (spilt_r - keep_r, spilt_c - keep_c))):
        slot_cols[:, i + 1 : i + 2] = UNITS * across(mine_c, r)
        slot_rows[i + 1 : i + 2, :] = UNITS * down(mine_r, c)


def make_plan(slot_expert):
    return pl.pallas_call(
        plan_kernel,
        out_shape=(
            jax.ShapeDtypeStruct((8, 128), jnp.int32),
            jax.ShapeDtypeStruct((8, 128), F32),
            jax.ShapeDtypeStruct((128, 8), F32),
        ),
        compiler_params=params(),
        name="plan",
    )(slot_expert.reshape(128, 1), slot_expert.reshape(1, 128))


def dispatch_kernel(tcol, trow, slot_rows, slot_cols, wrow, tok, cot, send, dest):
    sub, lane = grids()
    tc = [tcol[:, k : k + 1].astype(F32) for k in range(2)]
    tr = [trow[k : k + 1, :].astype(F32) for k in range(2)]
    dest_row = []
    for k in range(2):
        at = sub == tr[k]
        pos = down((tc[0] == tr[k]) & (sub < lane)) + down((tc[1] == tr[k]) & (sub < lane))
        slot, limit, first, rest = (down(at, slot_cols[:, i : i + 1]) for i in range(4))
        unit = slot + pos
        row = unit + jnp.where(unit < limit, first, rest)
        dest_row.append(jnp.where(pos < CAP, row, 4.0 * ROWS))
        at = lane == tc[k]
        pos = across((tc[k] == tr[0]) & (lane < sub)) + across((tc[k] == tr[1]) & (lane < sub))
        slot, limit, first, rest = (across(at, slot_rows[i : i + 1, :]) for i in range(4))
        unit = slot + pos
        row = unit + jnp.where(unit < limit, first, rest)
        dest[:, k : k + 1] = jnp.where(pos < CAP, row, 4.0 * ROWS)

    w0, w1 = wrow[0:1, :], wrow[1:2, :]
    for part in range(ROWS // 128):
        place = sub + 128.0 * part
        first, second = place == dest_row[0], place == dest_row[1]
        pick = jnp.where(first | second, 1.0, 0.0).astype(BF)
        weight = across(first, w0) + across(second, w1)
        rows = slice(part * 128, part * 128 + 128)
        send[rows, :D] = jnp.dot(pick, tok[...], preferred_element_type=F32).astype(BF)
        send[rows, D:] = (jnp.dot(pick, cot[...], preferred_element_type=F32) * weight).astype(BF)


def dispatch(targets, slot_rows, slot_cols, route_weight, tokens, cotangent):
    return pl.pallas_call(
        dispatch_kernel,
        out_shape=(
            jax.ShapeDtypeStruct((ROWS, 2 * D), BF),
            jax.ShapeDtypeStruct((128, 2), F32),
        ),
        compiler_params=params(),
        name="dispatch",
    )(targets, targets.T, slot_rows, slot_cols, route_weight.T, tokens, cotangent)


def picks(dest):
    place = lax.broadcasted_iota(jnp.int32, (128, ROWS), 1).astype(F32)
    return place == dest[:, 0:1], place == dest[:, 1:2]


def mix_kernel(dest, weight, cot, out, mixed, mix):
    first, second = picks(dest)
    pick0 = jnp.where(first, 1.0, 0.0).astype(BF)
    pick1 = jnp.where(second, 1.0, 0.0).astype(BF)
    w0, w1 = weight[:, 0:1], weight[:, 1:2]
    mix0 = jnp.zeros((128, 1), F32)
    mix1 = jnp.zeros((128, 1), F32)
    for c in range(0, D, 512):
        cols = slice(c, c + 512)
        out0, out1 = dot(pick0, out[:, cols]), dot(pick1, out[:, cols])
        here = cot[:, cols].astype(F32)
        mixed[:, cols] = (w0 * out0 + w1 * out1).astype(BF)
        mix0 += jnp.sum(here * out0, axis=1, keepdims=True)
        mix1 += jnp.sum(here * out1, axis=1, keepdims=True)
    mix[:, 0:1] = mix0
    mix[:, 1:2] = mix1


def mix_results(dest, route_weight, cotangent, back):
    return pl.pallas_call(
        mix_kernel,
        out_shape=(
            jax.ShapeDtypeStruct((128, D), BF),
            jax.ShapeDtypeStruct((128, 2), F32),
        ),
        compiler_params=params(),
        cost_estimate=LONG,
        name="mix_results",
    )(dest, route_weight, cotangent, back)


def add_kernel(dest, dx, grad):
    first, second = picks(dest)
    both = jnp.where(first | second, 1.0, 0.0).astype(BF)
    for c in range(0, D, 512):
        grad[:, c : c + 512] = dot(both, dx[:, c : c + 512]).astype(BF)


def add_gradients(dest, back):
    return pl.pallas_call(
        add_kernel,
        out_shape=jax.ShapeDtypeStruct((128, D), BF),
        compiler_params=params(),
        name="add_gradients",
    )(dest, back)


def prepare_kernel(core, w_in, w_out, mine, theirs):
    left_in, right_in = w_in[:, :, :HALF].astype(BF), w_in[:, :, HALF:].astype(BF)
    left_out, right_out = w_out[:, :, :HALF].astype(BF), w_out[:, :, HALF:].astype(BF)

    def put(left, right):
        left[:, :64], right[:, :64] = left_in, right_in
        left[:, 64:], right[:, 64:] = left_out, right_out

    @pl.when(core[0] == 0)
    def _():
        put(mine, theirs)

    @pl.when(core[0] != 0)
    def _():
        put(theirs, mine)


def prepare(core, w_in, w_out):
    n, r, c = w_in.shape
    ro = w_out.shape[1]
    half = pl.BlockSpec((n // 2, r + ro, HALF), lambda i, s: (i, 0, 0))
    return pl.pallas_call(
        prepare_kernel,
        grid_spec=pltpu.PrefetchScalarGridSpec(
            num_scalar_prefetch=1,
            grid=(2,),
            in_specs=[
                pl.BlockSpec((n // 2, r, c), lambda i, s: (i, 0, 0)),
                pl.BlockSpec((n // 2, ro, c), lambda i, s: (i, 0, 0)),
            ],
            out_specs=[half, half],
        ),
        out_shape=[jax.ShapeDtypeStruct((n, r + ro, HALF), BF)] * 2,
        compiler_params=params(),
        name="prepare",
    )(core, pltpu.with_memory_space_constraint(w_in, pltpu.HBM), pltpu.with_memory_space_constraint(w_out, pltpu.HBM))


def copy_one(e, parts, out, j):
    start = 0
    for part in parts:
        n = part.shape[0]

        @pl.when((e >= start) & (e < start + n))
        def _(start=start, n=n, part=part):
            out[j] = part[jnp.clip(e - start, 0, n - 1)]

        start += n


def take_kernel(index, mine, theirs, pair, cross):
    for j in range(FAR):
        copy_one(index[j], (mine, theirs), (pair, cross)[j // 2], j % 2)


def take_rows(index, mine, theirs):
    n, r, c = mine.shape
    whole = pl.BlockSpec((n, r, c), lambda i, s: (0, 0, 0))
    two = pl.BlockSpec((2, r, c), lambda i, s: (0, 0, 0))
    return pl.pallas_call(
        take_kernel,
        grid_spec=pltpu.PrefetchScalarGridSpec(
            num_scalar_prefetch=1, grid=(1,), in_specs=[whole] * 2, out_specs=[two] * 2
        ),
        out_shape=[jax.ShapeDtypeStruct((2, r, c), BF)] * 2,
        compiler_params=params(),
        name="take_rows",
    )(index, mine, theirs)


def select_kernel(index, *refs):
    step = pl.program_id(0)
    for j in range(8):
        copy_one(index[step * 8 + j], refs[:-1], refs[-1], j)


def select_rows(index, parts, start, r):
    c = parts[0].shape[2]
    return pl.pallas_call(
        select_kernel,
        grid_spec=pltpu.PrefetchScalarGridSpec(
            num_scalar_prefetch=1,
            grid=(4,),
            in_specs=[pl.BlockSpec((p.shape[0], r, c), lambda i, s: (0, start // r, 0)) for p in parts],
            out_specs=pl.BlockSpec((8, r, c), lambda i, s: (i, 0, 0)),
        ),
        out_shape=jax.ShapeDtypeStruct((32, r, c), BF),
        compiler_params=params(),
        name="select_rows",
    )(index, *parts)


def sum_kernel(index, rows, mine, theirs, pair, cross, total):
    total[...] = jnp.zeros_like(total)
    for d in range(32):
        e = index[d]
        total[e] += rows[d].astype(F32)
    mine[...] = total[:4].astype(BF)
    theirs[...] = total[4:8].astype(BF)
    pair[...] = total[8:10].astype(BF)
    cross[...] = total[10:].astype(BF)


def sum_rows(index, rows):
    n, r, c = rows.shape
    step = 16
    counts = (4, 4, 2, 2)
    return pl.pallas_call(
        sum_kernel,
        grid_spec=pltpu.PrefetchScalarGridSpec(
            num_scalar_prefetch=1,
            grid=(r // step,),
            in_specs=[pl.BlockSpec((n, step, c), lambda i, s: (0, i, 0))],
            out_specs=[pl.BlockSpec((k, step, c), lambda i, s: (0, i, 0)) for k in counts],
            scratch_shapes=[pltpu.VMEM((8 + FAR, step, c), F32)],
        ),
        out_shape=[jax.ShapeDtypeStruct((k, r, c), BF) for k in counts],
        compiler_params=params(),
        cost_estimate=LONG,
        name="sum_rows",
    )(index, rows)


def adam_kernel(sel, weight, moment, square, *refs):
    own, other = refs[:3], refs[3:6]
    new_w, new_m, new_s = refs[6:]
    rank = sel[1 + pl.program_id(0)]
    for h in range(2):
        cols = slice(h * HALF, (h + 1) * HALF)
        mine = sel[0] == h
        near, pair, cross = (jnp.where(mine, a[...], b[...]).astype(F32) for a, b in zip(own, other))
        grad = near + jnp.where(rank < 2, pair, jnp.where(rank < FAR, cross, 0.0))
        new_w[:, :, cols], new_m[:, :, cols], new_s[:, :, cols] = adam_step(
            weight[:, :, cols], moment[:, :, cols], square[:, :, cols], grad
        )


def adam(sel, weight, moment, square, own, other):
    n, r, c = weight.shape
    state = pl.BlockSpec((1, r, c), lambda i, s: (i, 0, 0))
    sums = [
        pl.BlockSpec((1, r, HALF), lambda i, s: (i, 0, 0)),
        pl.BlockSpec((1, r, HALF), lambda i, s: (jnp.clip(s[1 + i], 0, 1), 0, 0)),
        pl.BlockSpec((1, r, HALF), lambda i, s: (jnp.clip(s[1 + i] - 2, 0, 1), 0, 0)),
    ]
    return pl.pallas_call(
        adam_kernel,
        grid_spec=pltpu.PrefetchScalarGridSpec(
            num_scalar_prefetch=1,
            grid=(n,),
            in_specs=[state] * 3 + sums + sums,
            out_specs=[state] * 3,
        ),
        out_shape=[jax.ShapeDtypeStruct((n, r, c), F32)] * 3,
        compiler_params=params(),
        cost_estimate=LONG,
        name="adam",
    )(sel, weight, moment, square, *own, *other)


def rows_of(even, odd):
    return jnp.concatenate([w[0, i] for i in range(even.shape[1]) for w in (even, odd)], axis=0)


def halves(shape, place):
    return [
        pl.BlockSpec((1, *shape), lambda j, s: (s[1], *place(j))),
        pl.BlockSpec((1, *shape), lambda j, s: (1 - s[1], *place(j))),
    ]


def put_rows(out, v, flip):
    r = out.shape[2]
    for i in range(out.shape[1]):
        for y in range(2):
            out[y ^ flip, i] = v[(2 * i + y) * r : (2 * i + y + 1) * r].astype(BF)


def call(kernel, core, args, in_specs, out_shape, out_specs, steps, name, cost=SHORT):
    return pl.pallas_call(
        kernel,
        grid_spec=pltpu.PrefetchScalarGridSpec(
            num_scalar_prefetch=1, grid=(steps,), in_specs=in_specs, out_specs=out_specs
        ),
        out_shape=out_shape,
        compiler_params=params(56),
        cost_estimate=cost,
        name=name,
    )(core, *args)


def hidden_kernel(core, x, own0, own1, oth0, oth1, hidden, hidden_t, active, steep):
    one, two = dot(x[...], rows_of(own0, own1)), dot(x[...], rows_of(oth0, oth1))
    is0 = core[0] == 0
    gating, upward = jnp.where(is0, one, two), jnp.where(is0, two, one)
    logistic = jax.nn.sigmoid(gating)
    act = gating * logistic
    hid = act * upward
    hidden[...] = hid.astype(BF)
    hidden_t[...] = hid.T.astype(BF)
    active[...] = act
    steep[...] = upward * (logistic * (1.0 + gating * (1.0 - logistic)))


def other_hidden_kernel(core, x, own0, own1, oth0, oth1, hidden_t):
    one, two = dot(x[...], rows_of(own0, own1)), dot(x[...], rows_of(oth0, oth1))
    is0 = core[0] == 0
    gating, upward = jnp.where(is0, one, two), jnp.where(is0, two, one)
    hidden_t[...] = (gating * jax.nn.sigmoid(gating) * upward).T.astype(BF)


def other_hidden_of(core, got, own, oth):
    w = halves((16, 64, 256), lambda j: (0, 0, j))
    return call(
        other_hidden_kernel,
        core,
        (got, own, own, oth, oth),
        [pl.BlockSpec((ROWS, D), lambda j, s: (0, 0)), *w, *w],
        jax.ShapeDtypeStruct((FF, ROWS), BF),
        pl.BlockSpec((256, ROWS), lambda j, s: (j, 0)),
        FF // 256,
        "other_hidden",
    )


def hidden_of(core, got, own, oth):
    w = halves((16, 64, 256), lambda j: (0, 0, j))
    tile = pl.BlockSpec((ROWS, 256), lambda j, s: (0, j))
    return call(
        hidden_kernel,
        core,
        (got, own, own, oth, oth),
        [pl.BlockSpec((ROWS, D), lambda j, s: (0, 0)), *w, *w],
        [
            jax.ShapeDtypeStruct((ROWS, FF), BF),
            jax.ShapeDtypeStruct((FF, ROWS), BF),
            jax.ShapeDtypeStruct((ROWS, FF), F32),
            jax.ShapeDtypeStruct((ROWS, FF), F32),
        ],
        [tile, pl.BlockSpec((256, ROWS), lambda j, s: (j, 0)), tile, tile],
        FF // 256,
        "hidden",
    )


def outer_kernel(core, a_t, a2_t, b, b2, out):
    put_rows(out, dot(a_t[...], b[...]) + dot(a2_t[...], b2[...]), core[1])


def outer(core, a_t, a2_t, b, b2, place, name):
    m, k = a_t.shape
    left = pl.BlockSpec((m, k), lambda j, s: (0, 0))
    right = pl.BlockSpec((k, 256), lambda j, s: (0, 4 * place(s[0]) + j))
    return call(
        outer_kernel,
        core,
        (a_t, a2_t, b, b2),
        [left, left, right, right],
        jax.ShapeDtypeStruct((2, 16, m // 32, HALF), BF),
        pl.BlockSpec((2, 16, m // 32, 256), lambda j, s: (0, 0, 0, j)),
        4,
        name,
    )


def flip_kernel(core, one, two, one_t, two_t):
    one_t[...] = one[...].T
    two_t[...] = two[...].T


def flip(core, one, two):
    rows = pl.BlockSpec((ROWS, 512), lambda j, s: (0, j))
    return call(
        flip_kernel,
        core,
        (one, two),
        [rows, rows],
        [jax.ShapeDtypeStruct((D, ROWS), BF)] * 2,
        [pl.BlockSpec((512, ROWS), lambda j, s: (j, 0))] * 2,
        4,
        "flip",
        LONG,
    )


def back_kernel(core, dy_own, dy_oth, own0, own1, oth0, oth1, active, steep, d_own, d_oth):
    dhidden = dot_nt(dy_own[...], rows_of(own0, own1)) + dot_nt(dy_oth[...], rows_of(oth0, oth1))
    d_gate = (dhidden * steep[...]).astype(BF)
    d_up = (dhidden * active[...]).astype(BF)
    is0 = core[0] == 0
    d_own[...] = jnp.where(is0, d_gate, d_up)
    d_oth[...] = jnp.where(is0, d_up, d_gate)


def back_of(core, got, own, oth, active, steep):
    w = halves((4, 32, HALF), lambda j: (j, 0, 0))
    tile = pl.BlockSpec((ROWS, 256), lambda j, s: (0, j))
    return call(
        back_kernel,
        core,
        (got, got, own, own, oth, oth, active, steep),
        [
            pl.BlockSpec((ROWS, HALF), lambda j, s: (0, 2 + s[0])),
            pl.BlockSpec((ROWS, HALF), lambda j, s: (0, 3 - s[0])),
            *w,
            *w,
            tile,
            tile,
        ],
        [jax.ShapeDtypeStruct((ROWS, FF), BF)] * 2,
        [tile, tile],
        FF // 256,
        "back",
    )


def result_kernel(core, hidden, own0, own1, oth0, oth1, out):
    step = pl.program_id(0)

    @pl.when(step == 0)
    def _():
        out[...] = dot(hidden[...], rows_of(own0, own1)).astype(BF)

    @pl.when(step == 1)
    def _():
        out[...] = dot(hidden[...], rows_of(oth0, oth1)).astype(BF)


def result_of(core, hidden, own, oth):
    w = halves((16, 32, HALF), lambda j: (0, 0, 0))
    return call(
        result_kernel,
        core,
        (hidden, own, own, oth, oth),
        [pl.BlockSpec((ROWS, FF), lambda j, s: (0, 0)), *w, *w],
        jax.ShapeDtypeStruct((ROWS, D), BF),
        pl.BlockSpec((ROWS, HALF), lambda j, s: (0, jnp.where(j == 0, s[0], 1 - s[0]))),
        2,
        "result",
        LONG,
    )


def dx_kernel(core, d_own, d_oth, own0, own1, oth0, oth1, out):
    dx = dot_nt(d_own[...], rows_of(own0, own1)) + dot_nt(d_oth[...], rows_of(oth0, oth1))
    out[...] = dx.astype(BF)


def dx_of(core, d_own, d_oth, own, oth):
    row = pl.BlockSpec((ROWS, FF), lambda j, s: (0, 0))
    w = halves((4, 64, HALF), lambda j: (j, 0, 0))
    return call(
        dx_kernel,
        core,
        (d_own, d_oth, own, own, oth, oth),
        [row, row, *w, *w],
        jax.ShapeDtypeStruct((ROWS, D), BF),
        pl.BlockSpec((ROWS, 512), lambda j, s: (0, j)),
        4,
        "dx",
        LONG,
    )


def dot(a, b):
    return jnp.dot(a, b, preferred_element_type=F32)


def dot_nt(a, b):
    return lax.dot_general(a, b, (((1,), (1,)), ((), ())), preferred_element_type=F32)


def over_core(v):
    return lax.ppermute(v, "core", [(0, 1), (1, 0)])


def over_pair(v):
    return lax.ppermute(v, "yl", [(0, 1), (1, 0)])


def over_cross(v):
    return lax.ppermute(v, ("yl", "yh"), [(0, 3), (3, 0), (1, 2), (2, 1)])


def on_device(
    tokens,
    cotangent,
    route_weight,
    slot_expert,
    targets,
    proj_in,
    first_in,
    second_in,
    proj_out,
    first_out,
    second_out,
):
    core = lax.axis_index("core")
    yl = lax.axis_index("yl")
    which = core[None].astype(jnp.int32)

    def after(v, *first):
        return lax.optimization_barrier((v, *first))[0]

    def spread(v):
        got = lax.all_to_all(v.reshape(32, *v.shape[-2:]), SEND_AXES, split_axis=0, concat_axis=0, tiled=True)
        return got.reshape(2, 16, *v.shape[-2:])

    def exchange(v):
        return lax.all_to_all(
            v.reshape(CHIPS, UNITS, -1), CHIP_AXES, split_axis=0, concat_axis=0, tiled=True
        ).reshape(v.shape)

    plan, slot_rows, slot_cols = make_plan(slot_expert)

    rank, keep, spill, kept, spilt = (plan[i, :E] for i in range(5))
    ids = jnp.arange(E, dtype=jnp.int32)
    stored = (ids >> 3) == yl
    place = jnp.where(stored, (((ids >> 2) & 1) ^ core) * 4 + (ids & 3), 8 + rank)
    begin = jnp.where(stored, kept, spilt)
    length = jnp.where(stored, keep, spill)
    order = jnp.arange(HERE, dtype=jnp.int32)
    here = yl * HERE + ((order & 15) * 2 + (order >> 4))[:, None]
    index = jnp.sum(jnp.where((begin <= here) & (here < begin + length), place, 0), axis=1)
    ranked = stored & (rank == jnp.arange(FAR, dtype=jnp.int32)[:, None])
    largest = jnp.sum(jnp.where(ranked, place, 0), axis=1)
    own_rank = lax.dynamic_slice_in_dim(rank, (yl * 2 + core) * 4, 4)
    sel = jnp.concatenate([which, own_rank])

    mine, theirs = prepare(which, proj_in, proj_out)
    theirs = over_core(theirs)
    taken = take_rows(largest, mine, theirs)
    far = (over_pair(taken[0]), over_cross(taken[1]))
    send, dest = dispatch(targets, slot_rows, slot_cols, route_weight, after(tokens, *taken), cotangent)
    got = exchange(after(send, *far))
    for_in = select_rows(index, (mine, theirs, *far), 0, 64)
    for_out = select_rows(index, (mine, theirs, *far), 64, 32)
    for_in, for_out, got = lax.optimization_barrier((for_in, for_out, got))
    got2 = over_core(got)
    chip = lax.axis_index("yh") * 16 + lax.axis_index("x") * 4 + lax.axis_index("z")
    crossed = (lax.dynamic_index_in_dim(index, chip, keepdims=False) >= 10).astype(jnp.int32)
    which = jnp.stack([which[0], crossed])
    x_t, x2_t = flip(which, got, got2)
    own_in = spread(for_in)
    oth_in = over_core(own_in)
    own_out = spread(after(for_out, own_in))

    hidden, hidden_t, active, steep = hidden_of(which, got, own_in, oth_in)
    hidden2_t = other_hidden_of(which, got2, own_in, oth_in)
    grad_out = outer(which, hidden_t, hidden2_t, got, got2, lambda c: 2 + c, "outer_out")
    grad_out, own_out = lax.optimization_barrier((grad_out, own_out))
    oth_out = over_core(own_out)
    rows_out = spread(grad_out)

    d_own, d_oth = back_of(which, got, own_out, oth_out, after(active, grad_out), steep)
    d2_own = over_core(d_oth)
    grad_in = outer(which, x_t, x2_t, d_own, d2_own, lambda c: 0, "outer_in")
    rows_in = spread(after(grad_in, rows_out))

    def gather_sums(rows):
        near, near_other, pair, cross = sum_rows(index, rows.reshape(32, *rows.shape[2:]))
        pair, cross = over_pair(pair), over_cross(cross)
        own, other = (near, pair, cross), (over_core(near_other), over_core(pair), over_core(cross))
        return own, other

    result = result_of(which, hidden, own_out, oth_out)
    rows_dx = dx_of(which, d_own, d_oth, own_in, oth_in)
    own, other = gather_sums(after(rows_out, result, rows_dx))
    trained_out, mean_out, square_out = adam(sel, proj_out, first_out, second_out, own, other)
    rows_in = after(rows_in, result, rows_dx, *own)
    back = exchange(after(result, rows_in))
    own2, other2 = gather_sums(rows_in)
    mixed, mix_grad = mix_results(dest, route_weight, cotangent, back)
    back_dx = exchange(after(rows_dx, back))
    own2 = (after(own2[0], back), *own2[1:])
    trained_in, mean_in, square_in = adam(sel, proj_in, first_in, second_in, own2, other2)
    token_grad = add_gradients(dest, back_dx)
    return (
        mixed,
        token_grad,
        mix_grad,
        trained_in,
        mean_in,
        square_in,
        trained_out,
        mean_out,
        square_out,
    )


def solution(mesh):
    fine = Mesh(mesh.devices.reshape(2, 2, 4, 4, 2), ALL_AXES)
    rows = P(ALL_AXES, None)
    state = P(("yl", "core"), DEV_AXES, None)
    in_specs = (rows, rows, rows, P(), rows) + (state,) * 6
    out_specs = (rows, rows, rows) + (state,) * 6
    return jax.shard_map(on_device, mesh=fine, in_specs=in_specs, out_specs=out_specs, check_vma=False)
```

```python
import jax
import jax.numpy as jnp
from jax import lax
from jax.experimental import pallas as pl
from jax.experimental.pallas import tpu as pltpu
from jax.sharding import Mesh, PartitionSpec as P

D = 2048
FF = 1024
E = 16
CAP = 3
UNITS = 8
CHIPS = 64
ROWS = CHIPS * UNITS
HALF = 1024
HERE = 32
FAR = 4

BF = jnp.bfloat16
F32 = jnp.float32

beta_first = 0.9
beta_second = 0.95
learn_rate = 0.01
decay_rate = 0.1
adam_eps = 1e-08
bias_first = 1.0 - 0.9**10
bias_second = 1.0 - 0.95**10

CHIP_AXES = ("yl", "x", "z", "yh")
DEV_AXES = ("x", "z", "yh")
SEND_AXES = ("yh", "x", "z")
ALL_AXES = ("yl", "core", "x", "z", "yh")


def params(mib=48):
    return pltpu.CompilerParams(vmem_limit_bytes=mib * 2**20)


SHORT = pl.CostEstimate(flops=1, bytes_accessed=1, transcendentals=0)
LONG = pl.CostEstimate(flops=10**10, bytes_accessed=2 * 10**7, transcendentals=0)


def adam_step(weight, moment, square, gradient):
    new_moment = beta_first * moment + (1.0 - beta_first) * gradient
    new_square = beta_second * square + (1.0 - beta_second) * gradient * gradient
    update = (
        new_moment / bias_first / (jnp.sqrt(new_square / bias_second) + adam_eps)
        + decay_rate * weight
    )
    return (weight - learn_rate * update, new_moment, new_square)


def down(mask, value=1.0):
    return jnp.sum(jnp.where(mask, value, 0.0), axis=0, keepdims=True)


def across(mask, value=1.0):
    return jnp.sum(jnp.where(mask, value, 0.0), axis=1, keepdims=True)


def grids():
    sub = lax.broadcasted_iota(jnp.int32, (128, 128), 0).astype(F32)
    lane = lax.broadcasted_iota(jnp.int32, (128, 128), 1).astype(F32)
    return sub, lane


def plan_kernel(ecol, erow, plan, slot_rows, slot_cols):
    sub, lane = grids()
    ec, er = ecol[...].astype(F32), erow[...].astype(F32)

    chips_r = jnp.floor((CAP * down(ec == lane) + (UNITS - 1)) / UNITS)
    chips_c = jnp.floor((CAP * across(er == sub) + (UNITS - 1)) / UNITS)
    expert = (sub < E) & (lane < E)
    low_s, low_l = sub < E // 2, lane < E // 2
    same = expert & (low_s == low_l)
    ahead_r = same & ((chips_c > chips_r) | ((chips_c == chips_r) & (sub < lane)))
    ahead_c = same & ((chips_r > chips_c) | ((chips_r == chips_c) & (lane < sub)))
    rank_r = down(ahead_r)
    over_r = jnp.maximum(down(same, chips_c) - HERE, 0.0)
    over_c = jnp.maximum(across(same, chips_r) - HERE, 0.0)
    spill_r = jnp.clip(over_r - down(ahead_r, chips_c), 0.0, chips_r)
    spill_c = jnp.clip(over_c - across(ahead_c, chips_r), 0.0, chips_c)
    keep_r, keep_c = chips_r - spill_r, chips_c - spill_c
    across_y = expert & (low_s != low_l)
    kept_r = down(same & (sub < lane), keep_c)
    kept_c = across(same & (lane < sub), keep_r)
    spilt_r = down(across_y, keep_c) + down(same & (sub < lane), spill_c)
    spilt_c = across(across_y, keep_r) + across(same & (lane < sub), spill_r)
    y_r = jnp.where(low_l[0:1, :], 0.0, 1.0 * HERE)
    y_c = jnp.where(low_s[:, 0:1], 0.0, 1.0 * HERE)
    kept_r, kept_c = kept_r + y_r, kept_c + y_c
    spilt_r, spilt_c = spilt_r + (HERE - y_r), spilt_c + (HERE - y_c)
    for i, v in enumerate((rank_r, keep_r, spill_r, kept_r, spilt_r)):
        plan[i : i + 1, :] = v.astype(jnp.int32)

    mine_c, mine_r = ec == lane, er == sub
    slot_cols[:, 0:1] = CAP * across((ec == er) & (lane < sub))
    slot_rows[0:1, :] = CAP * down((ec == er) & (sub < lane))
    for i, (r, c) in enumerate(((keep_r, keep_c), (kept_r, kept_c), (spilt_r - keep_r, spilt_c - keep_c))):
        slot_cols[:, i + 1 : i + 2] = UNITS * across(mine_c, r)
        slot_rows[i + 1 : i + 2, :] = UNITS * down(mine_r, c)


def make_plan(slot_expert):
    return pl.pallas_call(
        plan_kernel,
        out_shape=(
            jax.ShapeDtypeStruct((8, 128), jnp.int32),
            jax.ShapeDtypeStruct((8, 128), F32),
            jax.ShapeDtypeStruct((128, 8), F32),
        ),
        compiler_params=params(),
        name="plan",
    )(slot_expert.reshape(128, 1), slot_expert.reshape(1, 128))


def dispatch_kernel(tcol, trow, slot_rows, slot_cols, wrow, tok, cot, send, dest):
    sub, lane = grids()
    tc = [tcol[:, k : k + 1].astype(F32) for k in range(2)]
    tr = [trow[k : k + 1, :].astype(F32) for k in range(2)]
    dest_row = []
    for k in range(2):
        at = sub == tr[k]
        pos = down((tc[0] == tr[k]) & (sub < lane)) + down((tc[1] == tr[k]) & (sub < lane))
        slot, limit, first, rest = (down(at, slot_cols[:, i : i + 1]) for i in range(4))
        unit = slot + pos
        row = unit + jnp.where(unit < limit, first, rest)
        dest_row.append(jnp.where(pos < CAP, row, 4.0 * ROWS))
        at = lane == tc[k]
        pos = across((tc[k] == tr[0]) & (lane < sub)) + across((tc[k] == tr[1]) & (lane < sub))
        slot, limit, first, rest = (across(at, slot_rows[i : i + 1, :]) for i in range(4))
        unit = slot + pos
        row = unit + jnp.where(unit < limit, first, rest)
        dest[:, k : k + 1] = jnp.where(pos < CAP, row, 4.0 * ROWS)

    w0, w1 = wrow[0:1, :], wrow[1:2, :]
    for part in range(ROWS // 128):
        place = sub + 128.0 * part
        first, second = place == dest_row[0], place == dest_row[1]
        pick = jnp.where(first | second, 1.0, 0.0).astype(BF)
        weight = across(first, w0) + across(second, w1)
        rows = slice(part * 128, part * 128 + 128)
        send[rows, :D] = jnp.dot(pick, tok[...], preferred_element_type=F32).astype(BF)
        send[rows, D:] = (jnp.dot(pick, cot[...], preferred_element_type=F32) * weight).astype(BF)


def dispatch(targets, slot_rows, slot_cols, route_weight, tokens, cotangent):
    return pl.pallas_call(
        dispatch_kernel,
        out_shape=(
            jax.ShapeDtypeStruct((ROWS, 2 * D), BF),
            jax.ShapeDtypeStruct((128, 2), F32),
        ),
        compiler_params=params(),
        name="dispatch",
    )(targets, targets.T, slot_rows, slot_cols, route_weight.T, tokens, cotangent)


def picks(dest):
    place = lax.broadcasted_iota(jnp.int32, (128, ROWS), 1).astype(F32)
    return place == dest[:, 0:1], place == dest[:, 1:2]


def mix_kernel(dest, weight, cot, out, mixed, mix):
    first, second = picks(dest)
    pick0 = jnp.where(first, 1.0, 0.0).astype(BF)
    pick1 = jnp.where(second, 1.0, 0.0).astype(BF)
    w0, w1 = weight[:, 0:1], weight[:, 1:2]
    mix0 = jnp.zeros((128, 1), F32)
    mix1 = jnp.zeros((128, 1), F32)
    for c in range(0, D, 512):
        cols = slice(c, c + 512)
        out0, out1 = dot(pick0, out[:, cols]), dot(pick1, out[:, cols])
        here = cot[:, cols].astype(F32)
        mixed[:, cols] = (w0 * out0 + w1 * out1).astype(BF)
        mix0 += jnp.sum(here * out0, axis=1, keepdims=True)
        mix1 += jnp.sum(here * out1, axis=1, keepdims=True)
    mix[:, 0:1] = mix0
    mix[:, 1:2] = mix1


def mix_results(dest, route_weight, cotangent, back):
    return pl.pallas_call(
        mix_kernel,
        out_shape=(
            jax.ShapeDtypeStruct((128, D), BF),
            jax.ShapeDtypeStruct((128, 2), F32),
        ),
        compiler_params=params(),
        cost_estimate=LONG,
        name="mix_results",
    )(dest, route_weight, cotangent, back)


def add_kernel(dest, dx, grad):
    first, second = picks(dest)
    both = jnp.where(first | second, 1.0, 0.0).astype(BF)
    for c in range(0, D, 512):
        grad[:, c : c + 512] = dot(both, dx[:, c : c + 512]).astype(BF)


def add_gradients(dest, back):
    return pl.pallas_call(
        add_kernel,
        out_shape=jax.ShapeDtypeStruct((128, D), BF),
        compiler_params=params(),
        name="add_gradients",
    )(dest, back)


def prepare_kernel(core, w_in, w_out, mine, theirs):
    left_in, right_in = w_in[:, :, :HALF].astype(BF), w_in[:, :, HALF:].astype(BF)
    left_out, right_out = w_out[:, :, :HALF].astype(BF), w_out[:, :, HALF:].astype(BF)

    def put(left, right):
        left[:, :64], right[:, :64] = left_in, right_in
        left[:, 64:], right[:, 64:] = left_out, right_out

    @pl.when(core[0] == 0)
    def _():
        put(mine, theirs)

    @pl.when(core[0] != 0)
    def _():
        put(theirs, mine)


def prepare(core, w_in, w_out):
    n, r, c = w_in.shape
    ro = w_out.shape[1]
    half = pl.BlockSpec((n // 2, r + ro, HALF), lambda i, s: (i, 0, 0))
    return pl.pallas_call(
        prepare_kernel,
        grid_spec=pltpu.PrefetchScalarGridSpec(
            num_scalar_prefetch=1,
            grid=(2,),
            in_specs=[
                pl.BlockSpec((n // 2, r, c), lambda i, s: (i, 0, 0)),
                pl.BlockSpec((n // 2, ro, c), lambda i, s: (i, 0, 0)),
            ],
            out_specs=[half, half],
        ),
        out_shape=[jax.ShapeDtypeStruct((n, r + ro, HALF), BF)] * 2,
        compiler_params=params(),
        name="prepare",
    )(core, pltpu.with_memory_space_constraint(w_in, pltpu.HBM), pltpu.with_memory_space_constraint(w_out, pltpu.HBM))


def copy_one(e, parts, out, j):
    start = 0
    for part in parts:
        n = part.shape[0]

        @pl.when((e >= start) & (e < start + n))
        def _(start=start, n=n, part=part):
            out[j] = part[jnp.clip(e - start, 0, n - 1)]

        start += n


def take_kernel(index, mine, theirs, pair, cross):
    for j in range(FAR):
        copy_one(index[j], (mine, theirs), (pair, cross)[j // 2], j % 2)


def take_rows(index, mine, theirs):
    n, r, c = mine.shape
    whole = pl.BlockSpec((n, r, c), lambda i, s: (0, 0, 0))
    two = pl.BlockSpec((2, r, c), lambda i, s: (0, 0, 0))
    return pl.pallas_call(
        take_kernel,
        grid_spec=pltpu.PrefetchScalarGridSpec(
            num_scalar_prefetch=1, grid=(1,), in_specs=[whole] * 2, out_specs=[two] * 2
        ),
        out_shape=[jax.ShapeDtypeStruct((2, r, c), BF)] * 2,
        compiler_params=params(),
        name="take_rows",
    )(index, mine, theirs)


def select_kernel(index, *refs):
    step = pl.program_id(0)
    for j in range(8):
        copy_one(index[step * 8 + j], refs[:-1], refs[-1], j)


def select_rows(index, parts, start, r):
    c = parts[0].shape[2]
    return pl.pallas_call(
        select_kernel,
        grid_spec=pltpu.PrefetchScalarGridSpec(
            num_scalar_prefetch=1,
            grid=(4,),
            in_specs=[pl.BlockSpec((p.shape[0], r, c), lambda i, s: (0, start // r, 0)) for p in parts],
            out_specs=pl.BlockSpec((8, r, c), lambda i, s: (i, 0, 0)),
        ),
        out_shape=jax.ShapeDtypeStruct((32, r, c), BF),
        compiler_params=params(),
        name="select_rows",
    )(index, *parts)


def sum_kernel(index, rows, mine, theirs, pair, cross, total):
    total[...] = jnp.zeros_like(total)
    for d in range(32):
        e = index[d]
        total[e] += rows[d].astype(F32)
    mine[...] = total[:4].astype(BF)
    theirs[...] = total[4:8].astype(BF)
    pair[...] = total[8:10].astype(BF)
    cross[...] = total[10:].astype(BF)


def sum_rows(index, rows):
    n, r, c = rows.shape
    step = 16
    counts = (4, 4, 2, 2)
    return pl.pallas_call(
        sum_kernel,
        grid_spec=pltpu.PrefetchScalarGridSpec(
            num_scalar_prefetch=1,
            grid=(r // step,),
            in_specs=[pl.BlockSpec((n, step, c), lambda i, s: (0, i, 0))],
            out_specs=[pl.BlockSpec((k, step, c), lambda i, s: (0, i, 0)) for k in counts],
            scratch_shapes=[pltpu.VMEM((8 + FAR, step, c), F32)],
        ),
        out_shape=[jax.ShapeDtypeStruct((k, r, c), BF) for k in counts],
        compiler_params=params(),
        cost_estimate=LONG,
        name="sum_rows",
    )(index, rows)


def adam_kernel(sel, weight, moment, square, *refs):
    own, other = refs[:3], refs[3:6]
    new_w, new_m, new_s = refs[6:]
    rank = sel[1 + pl.program_id(0)]
    for h in range(2):
        cols = slice(h * HALF, (h + 1) * HALF)
        mine = sel[0] == h
        near, pair, cross = (jnp.where(mine, a[...], b[...]).astype(F32) for a, b in zip(own, other))
        grad = near + jnp.where(rank < 2, pair, jnp.where(rank < FAR, cross, 0.0))
        new_w[:, :, cols], new_m[:, :, cols], new_s[:, :, cols] = adam_step(
            weight[:, :, cols], moment[:, :, cols], square[:, :, cols], grad
        )


def adam(sel, weight, moment, square, own, other):
    n, r, c = weight.shape
    state = pl.BlockSpec((1, r, c), lambda i, s: (i, 0, 0))
    sums = [
        pl.BlockSpec((1, r, HALF), lambda i, s: (i, 0, 0)),
        pl.BlockSpec((1, r, HALF), lambda i, s: (jnp.clip(s[1 + i], 0, 1), 0, 0)),
        pl.BlockSpec((1, r, HALF), lambda i, s: (jnp.clip(s[1 + i] - 2, 0, 1), 0, 0)),
    ]
    return pl.pallas_call(
        adam_kernel,
        grid_spec=pltpu.PrefetchScalarGridSpec(
            num_scalar_prefetch=1,
            grid=(n,),
            in_specs=[state] * 3 + sums + sums,
            out_specs=[state] * 3,
        ),
        out_shape=[jax.ShapeDtypeStruct((n, r, c), F32)] * 3,
        compiler_params=params(),
        cost_estimate=LONG,
        name="adam",
    )(sel, weight, moment, square, *own, *other)


def rows_of(even, odd):
    return jnp.concatenate([w[0, i] for i in range(even.shape[1]) for w in (even, odd)], axis=0)


def halves(shape, place):
    return [
        pl.BlockSpec((1, *shape), lambda j, s: (s[1], *place(j))),
        pl.BlockSpec((1, *shape), lambda j, s: (1 - s[1], *place(j))),
    ]


def put_rows(out, v, flip):
    r = out.shape[2]
    for i in range(out.shape[1]):
        for y in range(2):
            out[y ^ flip, i] = v[(2 * i + y) * r : (2 * i + y + 1) * r].astype(BF)


def call(kernel, core, args, in_specs, out_shape, out_specs, steps, name, cost=SHORT):
    return pl.pallas_call(
        kernel,
        grid_spec=pltpu.PrefetchScalarGridSpec(
            num_scalar_prefetch=1, grid=(steps,), in_specs=in_specs, out_specs=out_specs
        ),
        out_shape=out_shape,
        compiler_params=params(56),
        cost_estimate=cost,
        name=name,
    )(core, *args)


def hidden_kernel(core, x, own0, own1, oth0, oth1, hidden, hidden_t, active, steep):
    one, two = dot(x[...], rows_of(own0, own1)), dot(x[...], rows_of(oth0, oth1))
    is0 = core[0] == 0
    gating, upward = jnp.where(is0, one, two), jnp.where(is0, two, one)
    logistic = jax.nn.sigmoid(gating)
    act = gating * logistic
    hid = (act * upward).astype(BF)
    hidden[...] = hid
    hidden_t[...] = hid.T
    active[...] = act
    steep[...] = upward * (logistic * (1.0 + gating * (1.0 - logistic)))


def other_hidden_kernel(core, x, own0, own1, oth0, oth1, hidden_t):
    one, two = dot(x[...], rows_of(own0, own1)), dot(x[...], rows_of(oth0, oth1))
    is0 = core[0] == 0
    gating, upward = jnp.where(is0, one, two), jnp.where(is0, two, one)
    hidden_t[...] = (gating * jax.nn.sigmoid(gating) * upward).astype(BF).T


def other_hidden_of(core, got, own, oth):
    w = halves((16, 64, 256), lambda j: (0, 0, j))
    return call(
        other_hidden_kernel,
        core,
        (got, own, own, oth, oth),
        [pl.BlockSpec((ROWS, D), lambda j, s: (0, 0)), *w, *w],
        jax.ShapeDtypeStruct((FF, ROWS), BF),
        pl.BlockSpec((256, ROWS), lambda j, s: (j, 0)),
        FF // 256,
        "other_hidden",
    )


def hidden_of(core, got, own, oth):
    w = halves((16, 64, 256), lambda j: (0, 0, j))
    tile = pl.BlockSpec((ROWS, 256), lambda j, s: (0, j))
    return call(
        hidden_kernel,
        core,
        (got, own, own, oth, oth),
        [pl.BlockSpec((ROWS, D), lambda j, s: (0, 0)), *w, *w],
        [
            jax.ShapeDtypeStruct((ROWS, FF), BF),
            jax.ShapeDtypeStruct((FF, ROWS), BF),
            jax.ShapeDtypeStruct((ROWS, FF), F32),
            jax.ShapeDtypeStruct((ROWS, FF), F32),
        ],
        [tile, pl.BlockSpec((256, ROWS), lambda j, s: (j, 0)), tile, tile],
        FF // 256,
        "hidden",
    )


def outer_kernel(core, a_t, a2_t, b, b2, out):
    put_rows(out, dot(a_t[...], b[...]) + dot(a2_t[...], b2[...]), core[1])


def outer(core, a_t, a2_t, b, b2, place, name):
    m, k = a_t.shape
    left = pl.BlockSpec((m, k), lambda j, s: (0, 0))
    right = pl.BlockSpec((k, 256), lambda j, s: (0, 4 * place(s[0]) + j))
    return call(
        outer_kernel,
        core,
        (a_t, a2_t, b, b2),
        [left, left, right, right],
        jax.ShapeDtypeStruct((2, 16, m // 32, HALF), BF),
        pl.BlockSpec((2, 16, m // 32, 256), lambda j, s: (0, 0, 0, j)),
        4,
        name,
    )


def flip_kernel(core, one, two, one_t, two_t):
    one_t[...] = one[...].T
    two_t[...] = two[...].T


def flip(core, one, two):
    rows = pl.BlockSpec((ROWS, 512), lambda j, s: (0, j))
    return call(
        flip_kernel,
        core,
        (one, two),
        [rows, rows],
        [jax.ShapeDtypeStruct((D, ROWS), BF)] * 2,
        [pl.BlockSpec((512, ROWS), lambda j, s: (j, 0))] * 2,
        4,
        "flip",
        LONG,
    )


def back_kernel(core, dy_own, dy_oth, own0, own1, oth0, oth1, active, steep, d_own, d_oth):
    dhidden = dot_nt(dy_own[...], rows_of(own0, own1)) + dot_nt(dy_oth[...], rows_of(oth0, oth1))
    d_gate = (dhidden * steep[...]).astype(BF)
    d_up = (dhidden * active[...]).astype(BF)
    is0 = core[0] == 0
    d_own[...] = jnp.where(is0, d_gate, d_up)
    d_oth[...] = jnp.where(is0, d_up, d_gate)


def back_of(core, got, own, oth, active, steep):
    w = halves((4, 32, HALF), lambda j: (j, 0, 0))
    tile = pl.BlockSpec((ROWS, 256), lambda j, s: (0, j))
    return call(
        back_kernel,
        core,
        (got, got, own, own, oth, oth, active, steep),
        [
            pl.BlockSpec((ROWS, HALF), lambda j, s: (0, 2 + s[0])),
            pl.BlockSpec((ROWS, HALF), lambda j, s: (0, 3 - s[0])),
            *w,
            *w,
            tile,
            tile,
        ],
        [jax.ShapeDtypeStruct((ROWS, FF), BF)] * 2,
        [tile, tile],
        FF // 256,
        "back",
    )


def result_kernel(core, hidden, own0, own1, oth0, oth1, out):
    step = pl.program_id(0)

    @pl.when(step == 0)
    def _():
        out[...] = dot(hidden[...], rows_of(own0, own1)).astype(BF)

    @pl.when(step == 1)
    def _():
        out[...] = dot(hidden[...], rows_of(oth0, oth1)).astype(BF)


def result_of(core, hidden, own, oth):
    w = halves((16, 32, HALF), lambda j: (0, 0, 0))
    return call(
        result_kernel,
        core,
        (hidden, own, own, oth, oth),
        [pl.BlockSpec((ROWS, FF), lambda j, s: (0, 0)), *w, *w],
        jax.ShapeDtypeStruct((ROWS, D), BF),
        pl.BlockSpec((ROWS, HALF), lambda j, s: (0, jnp.where(j == 0, s[0], 1 - s[0]))),
        2,
        "result",
        LONG,
    )


def dx_kernel(core, d_own, d_oth, own0, own1, oth0, oth1, out):
    dx = dot_nt(d_own[...], rows_of(own0, own1)) + dot_nt(d_oth[...], rows_of(oth0, oth1))
    out[...] = dx.astype(BF)


def dx_of(core, d_own, d_oth, own, oth):
    row = pl.BlockSpec((ROWS, FF), lambda j, s: (0, 0))
    w = halves((4, 64, HALF), lambda j: (j, 0, 0))
    return call(
        dx_kernel,
        core,
        (d_own, d_oth, own, own, oth, oth),
        [row, row, *w, *w],
        jax.ShapeDtypeStruct((ROWS, D), BF),
        pl.BlockSpec((ROWS, 512), lambda j, s: (0, j)),
        4,
        "dx",
        LONG,
    )


def dot(a, b):
    return jnp.dot(a, b, preferred_element_type=F32)


def dot_nt(a, b):
    return lax.dot_general(a, b, (((1,), (1,)), ((), ())), preferred_element_type=F32)


def over_core(v):
    return lax.ppermute(v, "core", [(0, 1), (1, 0)])


def over_pair(v):
    return lax.ppermute(v, "yl", [(0, 1), (1, 0)])


def over_cross(v):
    return lax.ppermute(v, ("yl", "yh"), [(0, 3), (3, 0), (1, 2), (2, 1)])


def on_device(
    tokens,
    cotangent,
    route_weight,
    slot_expert,
    targets,
    proj_in,
    first_in,
    second_in,
    proj_out,
    first_out,
    second_out,
):
    core = lax.axis_index("core")
    yl = lax.axis_index("yl")
    which = core[None].astype(jnp.int32)

    def after(v, *first):
        return lax.optimization_barrier((v, *first))[0]

    def spread(v):
        got = lax.all_to_all(v.reshape(32, *v.shape[-2:]), SEND_AXES, split_axis=0, concat_axis=0, tiled=True)
        return got.reshape(2, 16, *v.shape[-2:])

    def exchange(v):
        return lax.all_to_all(
            v.reshape(CHIPS, UNITS, -1), CHIP_AXES, split_axis=0, concat_axis=0, tiled=True
        ).reshape(v.shape)

    plan, slot_rows, slot_cols = make_plan(slot_expert)

    rank, keep, spill, kept, spilt = (plan[i, :E] for i in range(5))
    ids = jnp.arange(E, dtype=jnp.int32)
    stored = (ids >> 3) == yl
    place = jnp.where(stored, (((ids >> 2) & 1) ^ core) * 4 + (ids & 3), 8 + rank)
    begin = jnp.where(stored, kept, spilt)
    length = jnp.where(stored, keep, spill)
    order = jnp.arange(HERE, dtype=jnp.int32)
    here = yl * HERE + ((order & 15) * 2 + (order >> 4))[:, None]
    index = jnp.sum(jnp.where((begin <= here) & (here < begin + length), place, 0), axis=1)
    ranked = stored & (rank == jnp.arange(FAR, dtype=jnp.int32)[:, None])
    largest = jnp.sum(jnp.where(ranked, place, 0), axis=1)
    own_rank = lax.dynamic_slice_in_dim(rank, (yl * 2 + core) * 4, 4)
    sel = jnp.concatenate([which, own_rank])

    mine, theirs = prepare(which, proj_in, proj_out)
    theirs = over_core(theirs)
    taken = take_rows(largest, mine, theirs)
    far = (over_pair(taken[0]), over_cross(taken[1]))
    send, dest = dispatch(targets, slot_rows, slot_cols, route_weight, after(tokens, *taken), cotangent)
    got = exchange(after(send, *far))
    for_in = select_rows(index, (mine, theirs, *far), 0, 64)
    for_out = select_rows(index, (mine, theirs, *far), 64, 32)
    for_in, for_out, got = lax.optimization_barrier((for_in, for_out, got))
    got2 = over_core(got)
    chip = lax.axis_index("yh") * 16 + lax.axis_index("x") * 4 + lax.axis_index("z")
    crossed = (lax.dynamic_index_in_dim(index, chip, keepdims=False) >= 10).astype(jnp.int32)
    which = jnp.stack([which[0], crossed])
    x_t, x2_t = flip(which, got, got2)
    own_in = spread(for_in)
    oth_in = over_core(own_in)
    own_out = spread(after(for_out, own_in))

    hidden, hidden_t, active, steep = hidden_of(which, got, own_in, oth_in)
    hidden2_t = other_hidden_of(which, got2, own_in, oth_in)
    grad_out = outer(which, hidden_t, hidden2_t, got, got2, lambda c: 2 + c, "outer_out")
    grad_out, own_out = lax.optimization_barrier((grad_out, own_out))
    oth_out = over_core(own_out)
    rows_out = spread(grad_out)

    d_own, d_oth = back_of(which, got, own_out, oth_out, after(active, grad_out), steep)
    d2_own = over_core(d_oth)
    grad_in = outer(which, x_t, x2_t, d_own, d2_own, lambda c: 0, "outer_in")
    rows_in = spread(after(grad_in, rows_out))

    def gather_sums(rows):
        near, near_other, pair, cross = sum_rows(index, rows.reshape(32, *rows.shape[2:]))
        pair, cross = over_pair(pair), over_cross(cross)
        own, other = (near, pair, cross), (over_core(near_other), over_core(pair), over_core(cross))
        return own, other

    result = result_of(which, hidden, own_out, oth_out)
    rows_dx = dx_of(which, d_own, d_oth, own_in, oth_in)
    own, other = gather_sums(after(rows_out, result, rows_dx))
    trained_out, mean_out, square_out = adam(sel, proj_out, first_out, second_out, own, other)
    rows_in = after(rows_in, result, rows_dx, *own)
    back = exchange(after(result, rows_in))
    own2, other2 = gather_sums(rows_in)
    mixed, mix_grad = mix_results(dest, route_weight, cotangent, back)
    back_dx = exchange(after(rows_dx, back))
    own2 = (after(own2[0], back), *own2[1:])
    trained_in, mean_in, square_in = adam(sel, proj_in, first_in, second_in, own2, other2)
    token_grad = add_gradients(dest, back_dx)
    return (
        mixed,
        token_grad,
        mix_grad,
        trained_in,
        mean_in,
        square_in,
        trained_out,
        mean_out,
        square_out,
    )


def solution(mesh):
    fine = Mesh(mesh.devices.reshape(2, 2, 4, 4, 2), ALL_AXES)
    rows = P(ALL_AXES, None)
    state = P(("yl", "core"), DEV_AXES, None)
    in_specs = (rows, rows, rows, P(), rows) + (state,) * 6
    out_specs = (rows, rows, rows) + (state,) * 6
    return jax.shard_map(on_device, mesh=fine, in_specs=in_specs, out_specs=out_specs, check_vma=False)
```
